256 devices in a mesh: pole: 4 (over x), row: 8 (over z_hi, core), col: 8 (over y, z_lo).
Axes of the slice: x: 4, y: 4, z: 8 (z_hi: 4, z_lo: 2; z = z_hi * 2 + z_lo), core: 2. Of those that a mesh axis runs over, the one named last changes fastest.
Arguments:
- root_inverse: float32 [4, 2, 4096, 4096], P('pole', None, 'row', 'col'), may hold values from -0.09375 to 0.09375
- panel: float32 [4, 2048, 2, 4096], P('pole', 'col', None, 'row'), may hold values from -2 to 2
- diag_inverse: float32 [4, 16, 2, 128, 128], P('pole', 'col'), may hold values from -4 to 4
- pole_weight: float32 [4, 2], P('pole'), may hold values from -3 to 3
- block_node: int32 [16], P('col'), may hold values from 0 to 3, as said below
- pattern: int32 [4, 32], P(None, 'row'), may hold values 0 or 1
Outputs:
- density_panel: float32 [2048, 4096], P('col', 'row')
- density_tiles: float32 [16, 128, 128], P('col')
The draws below stay inside these ranges and needn't reach their ends.
Inputs may be any that keep to these rules, and one draw needn't show every extreme that they name: `block_node`: each child supernode covers consecutive blocks, at least one and at most 8; one covers exactly 8.
All inputs are finite; a program needn't handle non-finite values. No bound on the sum of `pattern` on one device may be relied on, other than what follows from the above.
Results may differ from the reference program's by a relative error of at most 0.0001.
Values sent between devices are 32-bit elements; how exact they have to be, the bound alone decides.
A program may use at most 128 MiB of HBM per device.

```python
import jax
import jax.numpy as jnp
from jax import lax

R = 4096
TILE = 128
NODES = 4
POLES = 4
W = 2048
WB = 16
RB = 32
NODE_MOST = 8


def draw_block_node(key, part):
    key = jax.random.fold_in(key, 11)
    big_key, loop_key = jax.random.split(key)
    largest = jax.random.randint(big_key, (), 0, NODES).astype(jnp.int32)
    node_ids = jnp.arange(NODES, dtype=jnp.int32)
    is_big = node_ids == largest
    counts = jnp.where(is_big, NODE_MOST, 1).astype(jnp.int32)
    extra = WB - NODE_MOST - (NODES - 1)

    def place_one(step, state):
        running = state
        scores = jax.random.randint(jax.random.fold_in(loop_key, step), (NODES,), 0, 1 << 20).astype(jnp.int32)
        scores = scores * NODES + node_ids
        open_slot = jnp.logical_and(jnp.logical_not(is_big), running < NODE_MOST)
        scores = jnp.where(open_slot, scores, -1)
        chosen = jnp.argmax(scores).astype(jnp.int32)
        return running + (node_ids == chosen).astype(jnp.int32)
    counts = lax.fori_loop(0, extra, place_one, counts)
    bounds = jnp.cumsum(counts).astype(jnp.int32)
    positions = jnp.arange(WB, dtype=jnp.int32)
    return jnp.sum((positions[:, None] >= bounds[None, :NODES - 1]).astype(jnp.int32), axis=1).astype(jnp.int32)


def place_ends(drawn, rng, low, high):
    longest = drawn.shape.index(max(drawn.shape))
    spots = []
    for shift in (0, 1):
        where = [jax.random.randint(jax.random.fold_in(rng, axis), (), 0, length) for axis, length in enumerate(drawn.shape)]
        where[longest] = (where[longest] + shift) % drawn.shape[longest]
        spots.append(tuple(where))
    return drawn.at[spots[0]].set(low).at[spots[1]].set(high)


def levels(rng, extent, cuts, low, high):
    factor_of, own = 1.0, jax.random.fold_in(rng, 6)
    for dim, blocks in cuts:
        heights = jnp.exp(jax.random.uniform(jax.random.fold_in(own, dim), (blocks,), jnp.float32, low / len(cuts), high / len(cuts)))
        factor_of = factor_of * jnp.repeat(heights, extent[dim] // blocks).reshape([-1 if axis == dim else 1 for axis in range(len(extent))])
    return factor_of


def noise(rng, shape, deviation, reach, shards=(), kind=jnp.bfloat16):
    factor_of = levels(rng, shape, shards, -0.22, 0.18) if shards else 1.0
    result = jax.random.normal(rng, shape, jnp.float32) * deviation * factor_of
    return jnp.minimum(jnp.maximum(result, -reach), reach).astype(kind)


def setup_inputs(seed: int = 0) -> dict:
    keys = jax.random.split(jax.random.key(seed), 7)
    root_inverse = noise(keys[0], (POLES, 2, R, R), R ** -0.5, 0.09375, ((0, 4), (2, 8), (3, 8)), jnp.float32)
    panel = noise(keys[1], (POLES, W, 2, R), 0.125, 2.0, ((0, 4), (1, 8), (3, 8)), jnp.float32)
    diag_inverse = noise(keys[2], (POLES, WB, 2, TILE, TILE), 0.5, 4.0, ((0, 4), (1, 8)), jnp.float32)
    pole_weight = noise(keys[3], (POLES, 2), 1.0, 3.0, ((0, 4),), jnp.float32)
    block_node = draw_block_node(jax.random.fold_in(keys[6], 71), 0)
    pattern = place_ends((jax.random.randint(keys[5], (NODES, RB), 0, 4) < 3).astype(jnp.int32), jax.random.fold_in(keys[5], 1), 0, 1)
    return dict(root_inverse=root_inverse, panel=panel, diag_inverse=diag_inverse, pole_weight=pole_weight, block_node=block_node, pattern=pattern)


def contract(left, right):
    dims = (((1,), (1,)), ((), ()))
    return lax.dot_general(left, right, dims, precision=lax.Precision.HIGHEST, preferred_element_type=jnp.float32)


def apply_inverse(left_real, left_imag, inv_real, inv_imag):
    real_part = contract(left_real, inv_real) - contract(left_imag, inv_imag)
    imag_part = contract(left_imag, inv_real) + contract(left_real, inv_imag)
    return jnp.stack([real_part, imag_part], axis=1)


def tile_product(left, right):
    return jnp.einsum("tak,tbk->tab", left, right, precision=lax.Precision.HIGHEST)


def reference(root_inverse, panel, diag_inverse, pole_weight, block_node, pattern):
    node_hot = (block_node[:, None] == jnp.arange(NODES, dtype=jnp.int32)[None, :]).astype(jnp.float32)
    block_mask = jnp.dot(node_hot, pattern.astype(jnp.float32), precision=lax.Precision.HIGHEST)
    full_mask = jnp.repeat(jnp.repeat(block_mask, TILE, axis=0), TILE, axis=1)
    dens_panel = jnp.zeros((W, R), jnp.float32)
    dens_tiles = jnp.zeros((WB, TILE, TILE), jnp.float32)
    for which_pole in range(POLES):
        masked = panel[which_pole] * full_mask[:, None, :]
        product = apply_inverse(masked[:, 0], masked[:, 1], root_inverse[which_pole, 0], root_inverse[which_pole, 1])
        tiled_left = masked.reshape(WB, TILE, 2, R)
        tiled_right = product.reshape(WB, TILE, 2, R)
        coupling_real = tile_product(tiled_left[:, :, 0], tiled_right[:, :, 0]) - tile_product(tiled_left[:, :, 1], tiled_right[:, :, 1])
        coupling_imag = tile_product(tiled_left[:, :, 0], tiled_right[:, :, 1]) + tile_product(tiled_left[:, :, 1], tiled_right[:, :, 0])
        weight_real = pole_weight[which_pole, 0]
        weight_imag = pole_weight[which_pole, 1]
        dens_panel = dens_panel - (weight_real * product[:, 0] - weight_imag * product[:, 1]) * full_mask
        diag_block = diag_inverse[which_pole]
        dens_tiles = dens_tiles + weight_real * (diag_block[:, 0] + coupling_real) - weight_imag * (diag_block[:, 1] + coupling_imag)
    return dens_panel, dens_tiles
```

```python
import jax
import jax.numpy as jnp
from jax import lax
from jax.experimental import pallas as pl
from jax.experimental.pallas import tpu as pltpu
from jax.sharding import PartitionSpec as P

TILE = 128
NODES = 4
MESH = pl.DeviceIdType.MESH
HIGHEST = lax.Precision.HIGHEST
NT = (((1,), (1,)), ((), ()))
VMEM_LIMIT = 56 * 1024 * 1024


def wrap(index):
    return lax.rem(index + 8, 4)


def dot(left, right, precision=None):
    return lax.dot_general(left, right, NT, precision=precision, preferred_element_type=jnp.float32)


def split(value):
    high = value.astype(jnp.bfloat16)
    return high, (value - high.astype(jnp.float32)).astype(jnp.bfloat16)


def kernel(
    inv, pan, diag, mask, weight, dens, tiles,
    inv_all, pan_all, inv_split, pan_split, total, partial, pieces, summed, tile_parts,
    inv_send, inv_recv, pan_send, pan_recv, red_send, red_recv, tile_send, tile_recv,
    out_send, out_recv, tout_send, tout_recv, own_sem,
):
    p = lax.axis_index("pole")
    row = lax.axis_index("row")
    col = lax.axis_index("col")
    h, c = row // 2, row % 2
    y, l = col // 2, col % 2

    def at(p_, h_, c_, y_, l_):
        return (p_, 2 * h_ + c_, 2 * y_ + l_)

    def remote(source, target, send, recv, device):
        return pltpu.make_async_remote_copy(
            src_ref=source, dst_ref=target, send_sem=send, recv_sem=recv,
            device_id=device, device_id_type=MESH,
        )

    sibling = at(p, h, 1 - c, y, l)
    up, down = at(p, h, c, wrap(y + 1), l), at(p, h, c, wrap(y - 1), l)
    others = [at(p, wrap(h + d), k, y, l) for d in (1, 2, 3) for k in (0, 1)] + [sibling]
    reducers = [(wrap(p + d), (l + e) % 2) for d in range(4) for e in range(2)]

    barrier = pltpu.get_barrier_semaphore()
    greeted = [up, down] + others
    greeted += [at(p, wrap(h + l), k, y, 1 - l) for k in (0, 1)]
    greeted += [at(p, wrap(h - 1 + l), k, y, 1 - l) for k in (0, 1)]
    greeted += [at(wrap(p + d), h, c, y, k) for d in (1, 2, 3) for k in (0, 1)]
    for device in greeted:
        pl.semaphore_signal(barrier, inc=1, device_id=device, device_id_type=MESH)
    pl.semaphore_wait(barrier, len(greeted))

    started = []

    def send(*args):
        copy = remote(*args)
        copy.start()
        started.append(copy)

    first = [(0, up), (1, down), (1, up), (0, down)]
    own_slot = 2 * h + l
    same = 1 - (c - l) * (c - l)
    cross = 1 - same
    right_h = wrap(h + same + cross * l)
    left_h = wrap(h - 1 + cross * l)

    def send_inv(k):
        part, device = first[k]
        send(inv.at[part], inv_all.at[y, part], inv_send.at[k], inv_recv.at[y, part], device)

    def send_pan(k, half, h_):
        send(pan.at[half], pan_all.at[own_slot, half], pan_send.at[k], pan_recv.at[own_slot, half],
             at(p, h_, half, y, c))

    send_inv(0)
    send_inv(1)
    send_pan(0, 0, right_h)
    send_pan(1, 1, left_h)
    send_pan(2, 1, right_h)
    send_pan(3, 0, left_h)
    send_inv(2)
    send_inv(3)

    def shared(half):
        return remote(pan.at[half], pan_all.at[own_slot, half], pan_send.at[4 + half],
                      pan_recv.at[own_slot, half], sibling)

    def crossed(half):
        return remote(pan.at[half], pan_all.at[8, half], pan_send.at[6 + half],
                      pan_recv.at[8, half], at(p, h, c, y, 1 - l))

    @pl.when(same == 1)
    def _():
        for half in (0, 1):
            shared(half).start()
            pltpu.make_async_copy(pan.at[half], pan_all.at[own_slot, half], pan_recv.at[own_slot, half]).start()
        for half in (0, 1):
            crossed(half).start()

    own_inv = pltpu.make_async_copy(inv, inv_all.at[y], own_sem)
    own_inv.start()

    def arrived_inv(k, part):
        remote(inv.at[part], inv_all.at[k, part], inv_send.at[0], inv_recv.at[k, part], up).wait_recv()

    def arrived_pan(slot, half):
        remote(pan.at[half], pan_all.at[slot, half], pan_send.at[0], pan_recv.at[slot, half], sibling).wait_recv()

    y_left, y_right = wrap(y - 1), wrap(y + 1)
    cross_left = 2 * wrap(h - 1 + l) + 1 - l
    cross_right = 2 * wrap(h + l) + 1 - l
    same_left = 2 * wrap(h - 1) + l
    same_right = 2 * wrap(h + 1) + l
    far_left = 2 * wrap(h - 2 + l) + 1 - l
    far_right = 2 * wrap(h + 1 + l) + 1 - l
    same_far = 2 * wrap(h + 2) + l
    on_right, on_left = at(p, wrap(h + 1), c, y, l), at(p, wrap(h - 1), c, y, l)

    def pass_pan(k, slot, device):
        send(pan_all.at[slot, c], pan_all.at[slot, c], pan_send.at[k], pan_recv.at[slot, c], device)

    arrived_pan(cross_left, c)
    pass_pan(8, cross_left, on_right)
    pass_pan(9, cross_left, sibling)
    arrived_pan(cross_right, c)
    pass_pan(10, cross_right, on_left)
    pass_pan(11, cross_right, sibling)
    arrived_inv(y_left, 0)
    send(inv_all.at[y_left, 0], inv_all.at[y_left, 0], inv_send.at[4], inv_recv.at[y_left, 0], up)
    arrived_inv(y_right, 1)
    send(inv_all.at[y_right, 1], inv_all.at[y_right, 1], inv_send.at[5], inv_recv.at[y_right, 1], down)
    arrived_pan(same_left, c)
    arrived_pan(same_right, c)
    pass_pan(12, (1 - c) * same_left + c * same_right, at(p, wrap(h + 1 - 2 * c), c, y, l))
    pass_pan(13, same_left, sibling)
    pass_pan(14, same_right, sibling)

    own_inv.wait()
    arrived_pan(own_slot * same + (2 * h + l) * cross, 0)
    arrived_pan(own_slot * same + (2 * h + l) * cross, 1)
    for slot in (cross_left, cross_right, same_left, same_right):
        arrived_pan(slot, 1 - c)
    arrived_inv(y_left, 1)
    arrived_inv(y_right, 0)

    def multiply(k, fresh):
        def take(step, _):
            rows = pl.ds(pl.multiple_of(step * TILE, TILE), TILE)
            for part in (0, 1):
                high, low = split(inv_all[k, part, rows, :])
                inv_split[part, 0, rows, :] = high
                inv_split[part, 1, rows, :] = low
                high, low = split(pan_all[2 * k + step // 2, step % 2, part])
                pan_split[part, 0, rows, :] = high
                pan_split[part, 1, rows, :] = low
            return 0

        lax.fori_loop(0, 4, take, 0)

        def add(step, _):
            rows = pl.ds(pl.multiple_of(step * 256, 256), 256)

            def three(left, right):
                return (
                    dot(pan_split[left, 0], inv_split[right, 0, rows, :])
                    + dot(pan_split[left, 0], inv_split[right, 1, rows, :])
                    + dot(pan_split[left, 1], inv_split[right, 0, rows, :])
                )

            real = three(0, 0) - three(1, 1)
            imag = three(1, 0) + three(0, 1)
            if fresh:
                total[0, :, rows] = real
                total[1, :, rows] = imag
            else:
                total[0, :, rows] += real
                total[1, :, rows] += imag
            return 0

        lax.fori_loop(0, 2, add, 0)

    apart = (1 - lax.rem(h - y + 8, 2)) * (lax.rem(h - y + 8, 4) // 2)
    begin = wrap(h + apart * (2 * l - 1))
    multiply(begin, True)

    for k, slot in ((15, far_left), (16, far_right), (17, same_far)):
        arrived_pan(slot, c)
        pass_pan(k, slot, sibling)
    y_far = wrap(y + 2)
    arrived_inv(y_far, 0)
    arrived_inv(y_far, 1)
    for slot in (far_left, far_right, same_far):
        arrived_pan(slot, 1 - c)

    @pl.when(same == 0)
    def _():
        arrived_pan(8, 0)
        arrived_pan(8, 1)

    for d in (1, 2, 3):
        multiply(wrap(begin + d), False)

    real_weight = weight[0, 0]
    imag_weight = weight[0, 1]
    other = same * (2 * h + 1 - l) + cross * 8
    here = ((7 - row) // 7).astype(jnp.float32)
    for o in (0, 1):
        for half in (0, 1):
            begin_row = (l if o == 0 else 1 - l) * 256 + half * TILE
            rows = pl.ds(pl.multiple_of(begin_row, TILE), TILE)
            real = total[0, rows, :]
            imag = total[1, rows, :]
            weighted_real = real_weight * real - imag_weight * imag
            weighted_imag = real_weight * imag + imag_weight * real
            if o == 0:
                left_real, left_imag = pan[half, 0], pan[half, 1]
            else:
                left_real, left_imag = pan_all[other, half, 0], pan_all[other, half, 1]
            tile = dot(left_real, weighted_real, HIGHEST) - dot(left_imag, weighted_imag, HIGHEST)
            if o == 0:
                tile += here * (real_weight * diag[half, 0] - imag_weight * diag[half, 1])
            partial[rows, 0:512] = weighted_real
            partial[rows, 512:640] = tile

    me = 2 * p + l

    def piece(p_, l_):
        return pl.ds(pl.multiple_of(l_ * 256 + p_ * 64, 64), 64)

    for k in range(1, 8):
        p_, l_ = reducers[k]
        send(partial.at[piece(p_, l_)], pieces.at[me], red_send.at[k], red_recv.at[me], at(p_, h, c, y, l_))
    for k in range(1, 8):
        p_, l_ = reducers[k]
        remote(partial.at[piece(p_, l_)], pieces.at[2 * p_ + l_], red_send.at[k],
               red_recv.at[2 * p_ + l_], sibling).wait_recv()
    summed[...] = partial[piece(p, l), :]
    for k in range(1, 8):
        p_, l_ = reducers[k]
        summed[...] += pieces[2 * p_ + l_]

    tile_parts[row] = summed[:, 512:640]
    for k, device in enumerate(others):
        send(tile_parts.at[row], tile_parts.at[row], tile_send.at[k], tile_recv.at[row], device)
    mine = pl.ds(pl.multiple_of(p * 64, 64), 64)
    for j in range(4):
        dens[mine, j * TILE:(j + 1) * TILE] = -mask[p // 2, j] * summed[:, j * TILE:(j + 1) * TILE]
    for d in (1, 2, 3):
        send(dens.at[mine], dens.at[mine], out_send.at[d], out_recv.at[p], at(wrap(p + d), h, c, y, l))
    for k in range(1, 8):
        slot = lax.rem(row + k, 8)
        remote(tile_parts.at[slot], tile_parts.at[slot], tile_send.at[0], tile_recv.at[slot], sibling).wait_recv()
    whole = tile_parts[0]
    for k in range(1, 8):
        whole += tile_parts[k]
    tiles[mine, :] = whole
    for d in (1, 2, 3):
        send(tiles.at[mine], tiles.at[mine], tout_send.at[d], tout_recv.at[p], at(wrap(p + d), h, c, y, l))
    for d in (1, 2, 3):
        p_ = wrap(p + d)
        theirs = pl.ds(pl.multiple_of(p_ * 64, 64), 64)
        remote(dens.at[theirs], dens.at[theirs], out_send.at[0], out_recv.at[p_], sibling).wait_recv()
        remote(tiles.at[theirs], tiles.at[theirs], tout_send.at[0], tout_recv.at[p_], sibling).wait_recv()

    for copy in started:
        copy.wait_send()

    @pl.when(same == 1)
    def _():
        for half in (0, 1):
            shared(half).wait_send()
            crossed(half).wait_send()


def shards(root_inverse, panel, diag_inverse, pole_weight, block_node, pattern):
    node_hot = (block_node[:, None] == jnp.arange(NODES, dtype=jnp.int32)[None, :]).astype(jnp.float32)
    block_mask = jnp.sum(node_hot[:, :, None] * pattern.astype(jnp.float32)[None], axis=1)
    cut = panel[0].reshape(2, TILE, 2, 4, TILE) * block_mask[:, None, None, :, None]
    cut = cut.transpose(0, 2, 1, 3, 4).reshape(2, 2, TILE, 512)
    dma = pltpu.SemaphoreType.DMA
    vmem = pl.BlockSpec(memory_space=pltpu.VMEM)
    smem = pl.BlockSpec(memory_space=pltpu.SMEM)
    dens, tiles = pl.pallas_call(
        kernel,
        out_shape=(
            jax.ShapeDtypeStruct((256, 512), jnp.float32),
            jax.ShapeDtypeStruct((256, TILE), jnp.float32),
        ),
        in_specs=[pl.BlockSpec(memory_space=pl.ANY), vmem, vmem, smem, smem],
        out_specs=(vmem, vmem),
        scratch_shapes=[
            pltpu.VMEM((4, 2, 512, 512), jnp.float32),
            pltpu.VMEM((9, 2, 2, TILE, 512), jnp.float32),
            pltpu.VMEM((2, 2, 512, 512), jnp.bfloat16),
            pltpu.VMEM((2, 2, 512, 512), jnp.bfloat16),
            pltpu.VMEM((2, 512, 512), jnp.float32),
            pltpu.VMEM((512, 640), jnp.float32),
            pltpu.VMEM((8, 64, 640), jnp.float32),
            pltpu.VMEM((64, 640), jnp.float32),
            pltpu.VMEM((8, 64, TILE), jnp.float32),
            dma((6,)), dma((4, 2)),
            dma((18,)), dma((9, 2)),
            dma((8,)), dma((8,)),
            dma((7,)), dma((8,)),
            dma((4,)), dma((4,)),
            dma((4,)), dma((4,)),
            dma,
        ],
        compiler_params=pltpu.CompilerParams(
            collective_id=0, has_side_effects=True, vmem_limit_bytes=VMEM_LIMIT
        ),
        cost_estimate=pl.CostEstimate(flops=26_000_000_000, bytes_accessed=6_000_000, transcendentals=0),
    )(root_inverse[0], cut, diag_inverse[0], block_mask, pole_weight)
    return dens, tiles.reshape(2, TILE, TILE)


def solution(mesh):
    placed = (
        P("pole", None, "row", "col"),
        P("pole", "col", None, "row"),
        P("pole", "col", None, None, None),
        P("pole", None),
        P("col"),
        P(None, "row"),
    )
    return jax.shard_map(
        shards,
        mesh=mesh,
        in_specs=placed,
        out_specs=(P("col", "row"), P("col", None, None)),
        check_vma=False,
    )
```

```python
import jax
import jax.numpy as jnp
from jax import lax
from jax.experimental import pallas as pl
from jax.experimental.pallas import tpu as pltpu
from jax.sharding import PartitionSpec as P

TILE = 128
NODES = 4
MESH = pl.DeviceIdType.MESH
HIGHEST = lax.Precision.HIGHEST
NT = (((1,), (1,)), ((), ()))
VMEM_LIMIT = 60 * 1024 * 1024
F32 = jnp.float32
PAN_ROWS = (slice(0, 192), slice(192, 256))
INV_ROWS = (slice(0, 384), slice(384, 512))
PAN_GROUPS = ((0, 1, 2), (3,))
INV_GROUPS = ((0, 1, 2), (3,))


def wrap(index):
    return lax.rem(index + 8, 4)


def dot(left, right, precision=None):
    return lax.dot_general(left, right, NT, precision=precision, preferred_element_type=F32)


def split(value):
    high = value.astype(jnp.bfloat16)
    return high, (value - high.astype(F32)).astype(jnp.bfloat16)


def kernel(
    inv, panel, diag, weight, node, pattern, dens, tiles,
    raw, pan, inv_all, pan_all, inv_split, pan_split, real_part, imag_part, tile_part,
    early, early_sum, early_other, late_rows, late_cols, tile_pieces, tile_sum, tile_rows, tile_out,
    send_sem, inv_recv, pan_recv, early_recv, other_recv, rows_recv, cols_recv, piece_recv,
    part_recv, gather_recv, out_recv, own_sem,
):
    p = lax.axis_index("pole")
    row = lax.axis_index("row")
    col = lax.axis_index("col")
    h, c = row // 2, row % 2
    y, l = col // 2, col % 2
    same = 1 - (c - l) * (c - l)

    def at(p_, h_, c_, y_, l_):
        return (p_, 2 * h_ + c_, 2 * y_ + l_)

    sibling = at(p, h, 1 - c, y, l)
    partner = at(p, h, c, y, 1 - l)
    up, down = at(p, h, c, wrap(y + 1), l), at(p, h, c, wrap(y - 1), l)
    on_right, on_left = at(p, wrap(h + 1), c, y, l), at(p, wrap(h - 1), c, y, l)
    others = [(wrap(h + d), k) for d in (1, 2, 3) for k in (0, 1)] + [(h, 1 - c)]
    reducers = [(wrap(p + d), (l + e) % 2) for d in range(4) for e in range(2)][1:]
    poles = [wrap(p + d) for d in (1, 2, 3)]

    raw_copy = pltpu.make_async_copy(panel.at[0], raw, own_sem.at[1])
    raw_copy.start()
    own_inv = pltpu.make_async_copy(inv.at[0], inv_all.at[y], own_sem.at[0])
    own_inv.start()

    barrier = pltpu.get_barrier_semaphore()
    greeted = [up, down] + [at(p, h_, c_, y, l) for h_, c_ in others]
    greeted += [at(p, wrap(h + l), k, y, 1 - l) for k in (0, 1)]
    greeted += [at(p, wrap(h - 1 + l), k, y, 1 - l) for k in (0, 1)]
    greeted += [at(p_, h, c, y, k) for p_ in poles for k in (0, 1)]
    for device in greeted:
        pl.semaphore_signal(barrier, inc=1, device_id=device, device_id_type=MESH)
    pl.semaphore_wait(barrier, len(greeted))

    slots = [0]
    waits = []

    def remote(source, target, recv, device, slot):
        return pltpu.make_async_remote_copy(
            src_ref=source, dst_ref=target, send_sem=send_sem.at[slot], recv_sem=recv,
            device_id=device, device_id_type=MESH,
        )

    def fresh():
        slots[0] += 1
        return slots[0] - 1

    def send(source, target, recv, device):
        copy = remote(source, target, recv, device, fresh())
        copy.start()
        waits.append((None, copy.wait_send))

    def send_if(flag, jobs):
        kept = [(job, fresh()) for job in jobs]

        @pl.when(flag)
        def _():
            for job, slot in kept:
                remote(*job, slot).start()

        def finish():
            for job, slot in kept:
                remote(*job, slot).wait_send()

        waits.append((flag, finish))

    def arrived(target, recv):
        remote(target, target, recv, sibling, 0).wait_recv()

    def entry(block, j):
        value = jnp.int32(0)
        for n in range(NODES):
            value += jnp.where(node[block] == n, pattern[n, j], 0)
        return value.astype(F32)

    mask = [[entry(block, j) for j in range(4)] for block in range(2)]

    def inv_at(k, ri, part):
        return inv_all.at[k, ri, INV_ROWS[part], :], inv_recv.at[k, ri, part]

    def send_inv(part, ri, device):
        send(inv.at[0, ri, INV_ROWS[part], :], *inv_at(y, ri, part), device)

    def pass_inv(part, k, ri, device):
        target, recv = inv_at(k, ri, part)
        send(target, target, recv, device)

    def arrived_inv(part, k, ri):
        arrived(*inv_at(k, ri, part))

    def pan_at(slot, ri, part):
        return pan_all.at[slot, ri, PAN_ROWS[part], :], pan_recv.at[slot, ri, part]

    own_slot = 2 * h + l
    cross_left = 2 * wrap(h - 1 + l) + 1 - l
    cross_right = 2 * wrap(h + l) + 1 - l
    same_left = 2 * wrap(h - 1) + l
    same_right = 2 * wrap(h + 1) + l
    far_left = 2 * wrap(h - 2 + l) + 1 - l
    far_right = 2 * wrap(h + 1 + l) + 1 - l
    same_far = 2 * wrap(h + 2) + l
    behind = 2 * l - 1

    def send_pan(part):
        def job(ri, device):
            return (pan.at[ri, PAN_ROWS[part], :], *pan_at(own_slot, ri, part), device)

        send_if(same == 0, [
            job(ri, at(p, wrap(h + way + l), ri, y, 1 - l)) for ri in (0, 1) for way in (0, -1)
        ])
        crossed = [
            (pan.at[ri, PAN_ROWS[part], :], *pan_at(8, ri, part), partner) for ri in (0, 1)
        ]
        away = [job(ri, at(p, wrap(h + behind), ri, y, l)) for ri in (0, 1)]
        shared = [job(ri, sibling) for ri in (0, 1)]
        send_if(same == 1, crossed + away + shared)

        @pl.when(same == 1)
        def _():
            for ri in (0, 1):
                target, recv = pan_at(own_slot, ri, part)
                pltpu.make_async_copy(pan.at[ri, PAN_ROWS[part], :], target, recv).start()

    def pass_pan(part, slot, device):
        target, recv = pan_at(slot, c, part)
        send(target, target, recv, device)

    def arrived_pan(part, slot, ri):
        arrived(*pan_at(slot, ri, part))

    def pass_on(part):
        @pl.when(same == 0)
        def _():
            for ri in (0, 1):
                arrived_pan(part, 8, ri)

        send_if(same == 0, [
            (pan_at(8, ri, part)[0], *pan_at(2 * h + 1 - l, ri, part), at(p, wrap(h + behind), ri, y, 1 - l))
            for ri in (0, 1)
        ])
        arrived_pan(part, cross_left, c)
        pass_pan(part, cross_left, on_right)
        pass_pan(part, cross_left, sibling)
        arrived_pan(part, cross_right, c)
        pass_pan(part, cross_right, on_left)
        pass_pan(part, cross_right, sibling)
        arrived_inv(part, wrap(y - 1), 0)
        pass_inv(part, wrap(y - 1), 0, up)
        arrived_inv(part, wrap(y + 1), 1)
        pass_inv(part, wrap(y + 1), 1, down)
        arrived_pan(part, same_left, c)
        arrived_pan(part, same_right, c)
        pass_pan(part, (1 - c) * same_left + c * same_right, at(p, wrap(h + 1 - 2 * c), c, y, l))
        pass_pan(part, same_left, sibling)
        pass_pan(part, same_right, sibling)

    def split_inv(part, k):
        columns = pl.ds(pl.multiple_of(k * 512, 512), 512)
        for g in INV_GROUPS[part]:
            for ri in (0, 1):
                high, low = split(inv_all[k, ri, g * TILE:(g + 1) * TILE, :])
                inv_split[0, g, ri * TILE:(ri + 1) * TILE, columns] = high
                inv_split[1, g, ri * TILE:(ri + 1) * TILE, columns] = low

    def split_pan(part, slot):
        columns = pl.ds(pl.multiple_of((slot // 2) * 512, 512), 512)
        for g in PAN_GROUPS[part]:
            for ri in (0, 1):
                high, low = split(pan_all[slot, ri, g * 64:(g + 1) * 64, :])
                begin = ri * TILE + (slot % 2) * 64
                pan_split[g, pl.ds(pl.multiple_of(begin, 64), 64), columns] = high
                pan_split[g, pl.ds(pl.multiple_of(begin + 256, 64), 64), columns] = low

    def near(part):
        for slot in (own_slot,):
            arrived_pan(part, slot, 0)
            arrived_pan(part, slot, 1)
            split_pan(part, slot)
        for slot in (cross_left, cross_right, same_left, same_right):
            arrived_pan(part, slot, 1 - c)
            split_pan(part, slot)
        arrived_inv(part, wrap(y - 1), 1)
        split_inv(part, wrap(y - 1))
        arrived_inv(part, wrap(y + 1), 0)
        split_inv(part, wrap(y + 1))

    def far(part):
        for slot in (far_left, far_right, same_far):
            arrived_pan(part, slot, c)
            pass_pan(part, slot, sibling)
        k = wrap(y + 2)
        arrived_inv(part, k, 0)
        arrived_inv(part, k, 1)
        split_inv(part, k)
        for slot in (far_left, far_right, same_far):
            arrived_pan(part, slot, 1 - c)
            split_pan(part, slot)

    real_weight = weight[0, 0]
    imag_weight = weight[0, 1]

    def multiply(g, block):
        both = dot(pan_split[g], inv_split[0, block])
        rest = dot(pan_split[g, 0:256, :], inv_split[1, block])
        from_real = both[0:TILE] + both[256:384] + rest[0:TILE]
        from_imag = both[TILE:256] + both[384:512] + rest[TILE:256]
        real = from_real[:, 0:TILE] - from_imag[:, TILE:256]
        imag = from_imag[:, 0:TILE] + from_real[:, TILE:256]
        weighted_real = real_weight * real - imag_weight * imag
        weighted_imag = real_weight * imag + imag_weight * real
        rows = pl.ds(pl.multiple_of(g * 64, 64), 64)
        columns = pl.ds(pl.multiple_of(block * TILE, TILE), TILE)
        for k in (0, 1):
            real_part[k, rows, columns] = weighted_real[k * 64:(k + 1) * 64]
            imag_part[k, rows, columns] = weighted_imag[k * 64:(k + 1) * 64]

    def loop(begin, end, body):
        def step(i, _):
            body(i)
            return 0

        lax.fori_loop(begin, end, step, 0)

    def multiply_early(i):
        multiply(i // 3, i % 3)

    send_inv(0, 0, up)
    send_inv(0, 1, down)
    send_inv(0, 1, up)
    send_inv(0, 0, down)
    raw_copy.wait()
    for part in (0, 1):
        for g in PAN_GROUPS[part]:
            rows = slice(g * 64, (g + 1) * 64)
            for ri in (0, 1):
                value = raw[rows, ri, :]
                for j in range(4):
                    columns = slice(j * TILE, (j + 1) * TILE)
                    pan[ri, rows, columns] = value[:, columns] * mask[g // 2][j]
        if part == 0:
            send_pan(0)
    own_inv.wait()
    split_inv(0, y)
    split_inv(1, y)
    pass_on(0)
    send_inv(1, 0, up)
    send_inv(1, 1, down)
    send_pan(1)
    send_inv(1, 1, up)
    send_inv(1, 0, down)
    near(0)
    far(0)

    loop(0, 4, multiply_early)
    pass_on(1)
    loop(4, 9, multiply_early)

    rows_first = pl.ds(pl.multiple_of(p * 48, 16), 48)
    rows_last = pl.ds(pl.multiple_of(192 + p * 16, 16), 16)

    def first_of(p_):
        return pl.ds(pl.multiple_of(p_ * 48, 16), 48)

    def last_of(p_):
        return pl.ds(pl.multiple_of(192 + p_ * 16, 16), 16)

    for p_ in poles:
        send(real_part.at[:, first_of(p_), 0:384], early.at[p], early_recv.at[p], at(p_, h, c, y, l))
    near(1)
    early_sum[...] = real_part[:, rows_first, 0:384]
    for p_ in poles:
        arrived(early.at[p_], early_recv.at[p_])
        early_sum[...] += early[p_]
    send(early_sum.at[1 - l], early_other, other_recv, partner)
    far(1)
    arrived(early_other, other_recv)

    def masked(total, begin, columns):
        upper = begin // TILE
        for j in columns:
            wide = slice((j - columns[0]) * TILE, (j - columns[0] + 1) * TILE)
            factor = jnp.where(upper == 0, mask[0][j], mask[1][j])
            dens[pl.ds(pl.multiple_of(begin, 16), 16), j * TILE:(j + 1) * TILE] = -factor * total[:, wide]

    for s in range(3):
        inner = slice(s * 16, (s + 1) * 16)
        masked(early_sum[l, inner, :] + early_other[inner, :], p * 48 + s * 16, (0, 1, 2))
    for p_ in poles:
        send(dens.at[rows_first, 0:384], dens.at[rows_first, 0:384], out_recv.at[p, 0], at(p_, h, c, y, l))

    me = 2 * p + l
    loop(0, 4, lambda i: multiply(3, i))
    for p_, l_ in reducers:
        send(real_part.at[l_, last_of(p_), :], late_rows.at[me], rows_recv.at[me], at(p_, h, c, y, l_))
    loop(0, 3, lambda i: multiply(i, 3))
    for p_, l_ in reducers:
        send(real_part.at[l_, first_of(p_), 384:512], late_cols.at[me], cols_recv.at[me], at(p_, h, c, y, l_))

    other = same * (2 * h + 1 - l) + (1 - same) * 8
    here = ((7 - row) // 7).astype(F32)
    for o in (0, 1):
        for half in (0, 1):
            inner = slice(half * TILE, (half + 1) * TILE)
            k = l if o == 0 else 1 - l
            left = (pan, pan_all.at[other])[o]
            tile = dot(left[0, inner, :], real_part[k, inner, :], HIGHEST)
            tile -= dot(left[1, inner, :], imag_part[k, inner, :], HIGHEST)
            if o == 0:
                tile += here * (real_weight * diag[0, half, 0] - imag_weight * diag[0, half, 1])
            tile_part[k, inner, :] = tile

    def quarter(p_):
        return pl.ds(pl.multiple_of(p_ * 64, 64), 64)

    for p_, l_ in reducers:
        send(tile_part.at[l_, quarter(p_), :], tile_pieces.at[me], piece_recv.at[me], at(p_, h, c, y, l_))

    def collect(own, buffer, recv):
        total = own
        for p_, l_ in reducers:
            k = 2 * p_ + l_
            arrived(buffer.at[k], recv.at[k])
            total += buffer[k]
        return total

    masked(collect(real_part[l, rows_last, :], late_rows, rows_recv), 192 + p * 16, (0, 1, 2, 3))
    for p_ in poles:
        send(dens.at[rows_last, :], dens.at[rows_last, :], out_recv.at[p, 1], at(p_, h, c, y, l))
    total = collect(real_part[l, rows_first, 384:512], late_cols, cols_recv)
    for s in range(3):
        masked(total[s * 16:(s + 1) * 16], p * 48 + s * 16, (3,))
    for p_ in poles:
        send(dens.at[rows_first, 384:512], dens.at[rows_first, 384:512], out_recv.at[p, 2], at(p_, h, c, y, l))

    tile_sum[...] = collect(tile_part[l, quarter(p), :], tile_pieces, piece_recv)

    def eighth(k):
        return pl.ds(pl.multiple_of(k * 8, 8), 8)

    for h_, c_ in others:
        send(tile_sum.at[eighth(2 * h_ + c_), :], tile_rows.at[row], part_recv.at[row], at(p, h_, c_, y, l))
    total = tile_sum[eighth(row), :]
    for h_, c_ in others:
        k = 2 * h_ + c_
        arrived(tile_rows.at[k], part_recv.at[k])
        total += tile_rows[k]
    tile_out[eighth(row), :] = total
    for h_, c_ in others:
        send(tile_out.at[eighth(row), :], tile_out.at[eighth(row), :], gather_recv.at[row], at(p, h_, c_, y, l))
    for h_, c_ in others:
        k = 2 * h_ + c_
        arrived(tile_out.at[eighth(k), :], gather_recv.at[k])
    tiles[quarter(p), :] = tile_out[...]
    for p_ in poles:
        send(tiles.at[quarter(p), :], tiles.at[quarter(p), :], out_recv.at[p, 3], at(p_, h, c, y, l))
    for p_ in poles:
        for k, target in enumerate((
            dens.at[first_of(p_), 0:384], dens.at[last_of(p_), :], dens.at[first_of(p_), 384:512],
            tiles.at[quarter(p_), :],
        )):
            arrived(target, out_recv.at[p_, k])

    for flag, finish in waits:
        if flag is None:
            finish()
        else:
            pl.when(flag)(finish)


def shards(root_inverse, panel, diag_inverse, pole_weight, block_node, pattern):
    dma = pltpu.SemaphoreType.DMA
    vmem = pl.BlockSpec(memory_space=pltpu.VMEM)
    smem = pl.BlockSpec(memory_space=pltpu.SMEM)
    hbm = pl.BlockSpec(memory_space=pl.ANY)
    half = jnp.bfloat16
    dens, tiles = pl.pallas_call(
        kernel,
        out_shape=(jax.ShapeDtypeStruct((256, 512), F32), jax.ShapeDtypeStruct((256, TILE), F32)),
        in_specs=[hbm, hbm, vmem, smem, smem, smem],
        out_specs=(vmem, vmem),
        scratch_shapes=[
            pltpu.VMEM((256, 2, 512), F32),
            pltpu.VMEM((2, 256, 512), F32),
            pltpu.VMEM((4, 2, 512, 512), F32),
            pltpu.VMEM((9, 2, 256, 512), F32),
            pltpu.VMEM((2, 4, 256, 2048), half),
            pltpu.VMEM((4, 512, 2048), half),
            pltpu.VMEM((2, 256, 512), F32),
            pltpu.VMEM((2, 256, 512), F32),
            pltpu.VMEM((2, 256, TILE), F32),
            pltpu.VMEM((4, 2, 48, 384), F32),
            pltpu.VMEM((2, 48, 384), F32),
            pltpu.VMEM((48, 384), F32),
            pltpu.VMEM((8, 16, 512), F32),
            pltpu.VMEM((8, 48, TILE), F32),
            pltpu.VMEM((8, 64, TILE), F32),
            pltpu.VMEM((64, TILE), F32),
            pltpu.VMEM((8, 8, TILE), F32),
            pltpu.VMEM((64, TILE), F32),
            dma((128,)),
            dma((4, 2, 2)), dma((9, 2, 2)),
            dma((4,)), dma, dma((8,)), dma((8,)), dma((8,)),
            dma((8,)), dma((8,)), dma((4, 4)), dma((2,)),
        ],
        compiler_params=pltpu.CompilerParams(
            collective_id=0, has_side_effects=True, vmem_limit_bytes=VMEM_LIMIT
        ),
        cost_estimate=pl.CostEstimate(flops=26_000_000_000, bytes_accessed=6_000_000, transcendentals=0),
    )(root_inverse, panel, diag_inverse, pole_weight, block_node, pattern)
    return dens, tiles.reshape(2, TILE, TILE)


def solution(mesh):
    placed = (
        P("pole", None, "row", "col"),
        P("pole", "col", None, "row"),
        P("pole", "col", None, None, None),
        P("pole", None),
        P("col"),
        P(None, "row"),
    )
    return jax.shard_map(
        shards,
        mesh=mesh,
        in_specs=placed,
        out_specs=(P("col", "row"), P("col", None, None)),
        check_vma=False,
    )
```

```python
import jax
import jax.numpy as jnp
from jax import lax
from jax.experimental import pallas as pl
from jax.experimental.pallas import tpu as pltpu
from jax.sharding import PartitionSpec as P

TILE = 128
NODES = 4
MESH = pl.DeviceIdType.MESH
HIGHEST = lax.Precision.HIGHEST
NT = (((1,), (1,)), ((), ()))
VMEM_LIMIT = 60 * 1024 * 1024
F32 = jnp.float32
PARTS = 4
SENDS = 320


def wrap(index):
    return lax.rem(index + 8, 4)


def dot(left, right, precision=None):
    return lax.dot_general(left, right, NT, precision=precision, preferred_element_type=F32)


def split(value):
    high = value.astype(jnp.bfloat16)
    return high, (value - high.astype(F32)).astype(jnp.bfloat16)


def kernel(
    inv, panel, diag, weight, node, pattern, dens, tiles,
    raw, pan, inv_all, pan_all, inv_split, pan_split, begun, real_part, left_split, right_split, tile_part,
    early, early_sum, early_other, late_rows, late_cols, tile_other, tile_sum, tile_pieces, tile_rows,
    send_sem, inv_recv, pan_recv, early_recv, other_recv, rows_recv, cols_recv, core_recv, piece_recv,
    part_recv, out_recv, tile_recv, own_sem,
):
    p = lax.axis_index("pole")
    row = lax.axis_index("row")
    col = lax.axis_index("col")
    h, c = row // 2, row % 2
    y, l = col // 2, col % 2
    same = 1 - (c - l) * (c - l)

    def at(p_, h_, c_, y_, l_):
        return (p_, 2 * h_ + c_, 2 * y_ + l_)

    sibling = at(p, h, 1 - c, y, l)
    partner = at(p, h, c, y, 1 - l)
    up, down = at(p, h, c, wrap(y + 1), l), at(p, h, c, wrap(y - 1), l)
    on_right, on_left = at(p, wrap(h + 1), c, y, l), at(p, wrap(h - 1), c, y, l)
    others = [(wrap(h + d), k) for d in (1, 2, 3) for k in (0, 1)] + [(h, 1 - c)]
    heights = [wrap(h + d) for d in (1, 2, 3)]
    reducers = [(wrap(p + d), (l + e) % 2) for d in range(4) for e in range(2)][1:]
    poles = [wrap(p + d) for d in (1, 2, 3)]
    copies = [(p_, c_) for p_ in poles for c_ in (c, 1 - c)] + [(p, 1 - c)]

    raw_copy = pltpu.make_async_copy(panel.at[0], raw, own_sem.at[1])
    raw_copy.start()
    own_inv = pltpu.make_async_copy(inv.at[0], inv_all.at[y], own_sem.at[0])
    own_inv.start()

    barrier = pltpu.get_barrier_semaphore()
    greeted = [up, down] + [at(p, h_, c_, y, l) for h_, c_ in others]
    greeted += [at(p, wrap(h + l), k, y, 1 - l) for k in (0, 1)]
    greeted += [at(p, wrap(h - 1 + l), k, y, 1 - l) for k in (0, 1)]
    greeted += [at(p_, h, c, y, k) for p_ in poles for k in (0, 1)]
    greeted += [at(p_, h, 1 - c, y, l) for p_ in poles]
    for device in greeted:
        pl.semaphore_signal(barrier, inc=1, device_id=device, device_id_type=MESH)

    slots = [0]
    waits = []

    def remote(source, target, recv, device, slot):
        return pltpu.make_async_remote_copy(
            src_ref=source, dst_ref=target, send_sem=send_sem.at[slot], recv_sem=recv,
            device_id=device, device_id_type=MESH,
        )

    def fresh():
        slots[0] += 1
        return slots[0] - 1

    def send(source, target, recv, device):
        copy = remote(source, target, recv, device, fresh())
        copy.start()
        waits.append((None, copy.wait_send))

    def send_if(flag, jobs):
        kept = [(job, fresh()) for job in jobs]

        @pl.when(flag)
        def _():
            for job, slot in kept:
                remote(*job, slot).start()

        def finish():
            for job, slot in kept:
                remote(*job, slot).wait_send()

        waits.append((flag, finish))

    def arrived(target, recv):
        remote(target, target, recv, sibling, 0).wait_recv()

    def entry(block, j):
        value = jnp.int32(0)
        for n in range(NODES):
            value += jnp.where(node[block] == n, pattern[n, j], 0)
        return value.astype(F32)

    mask = [[entry(block, j) for j in range(4)] for block in range(2)]

    def inv_at(k, ri, part):
        return inv_all.at[k, ri, pl.ds(part * TILE, TILE), :], inv_recv.at[k, ri, part]

    def send_inv(part, ri, device):
        send(inv.at[0, ri, pl.ds(part * TILE, TILE), :], *inv_at(y, ri, part), device)

    def pass_inv(part, k, ri, device):
        target, recv = inv_at(k, ri, part)
        send(target, target, recv, device)

    def arrived_inv(part, k, ri):
        arrived(*inv_at(k, ri, part))

    def pan_at(slot, ri, part):
        return pan_all.at[slot, ri, pl.ds(part * 64, 64), :], pan_recv.at[slot, ri, part]

    own_slot = 2 * h + l
    cross_left = 2 * wrap(h - 1 + l) + 1 - l
    cross_right = 2 * wrap(h + l) + 1 - l
    same_left = 2 * wrap(h - 1) + l
    same_right = 2 * wrap(h + 1) + l
    far_left = 2 * wrap(h - 2 + l) + 1 - l
    far_right = 2 * wrap(h + 1 + l) + 1 - l
    same_far = 2 * wrap(h + 2) + l
    behind = 2 * l - 1

    def send_pan(part):
        def job(ri, device):
            return (pan.at[ri, pl.ds(part * 64, 64), :], *pan_at(own_slot, ri, part), device)

        send_if(same == 0, [
            job(ri, at(p, wrap(h + way + l), ri, y, 1 - l)) for ri in (0, 1) for way in (0, -1)
        ])
        crossed = [
            (pan.at[ri, pl.ds(part * 64, 64), :], *pan_at(8, ri, part), partner) for ri in (0, 1)
        ]
        away = [job(ri, at(p, wrap(h + behind), ri, y, l)) for ri in (0, 1)]
        shared = [job(ri, sibling) for ri in (0, 1)]
        send_if(same == 1, crossed + away + shared)

        @pl.when(same == 1)
        def _():
            for ri in (0, 1):
                target, recv = pan_at(own_slot, ri, part)
                pltpu.make_async_copy(pan.at[ri, pl.ds(part * 64, 64), :], target, recv).start()

    def pass_pan(part, slot, device):
        target, recv = pan_at(slot, c, part)
        send(target, target, recv, device)

    def arrived_pan(part, slot, ri):
        arrived(*pan_at(slot, ri, part))

    def pass_on(part):
        @pl.when(same == 0)
        def _():
            for ri in (0, 1):
                arrived_pan(part, 8, ri)

        send_if(same == 0, [
            (pan_at(8, ri, part)[0], *pan_at(2 * h + 1 - l, ri, part), at(p, wrap(h + behind), ri, y, 1 - l))
            for ri in (0, 1)
        ])
        arrived_pan(part, cross_left, c)
        pass_pan(part, cross_left, on_right)
        pass_pan(part, cross_left, sibling)
        arrived_pan(part, cross_right, c)
        pass_pan(part, cross_right, on_left)
        pass_pan(part, cross_right, sibling)
        arrived_inv(part, wrap(y - 1), 0)
        pass_inv(part, wrap(y - 1), 0, up)
        arrived_inv(part, wrap(y + 1), 1)
        pass_inv(part, wrap(y + 1), 1, down)

    def pass_same(part):
        arrived_pan(part, same_left, c)
        arrived_pan(part, same_right, c)
        pass_pan(part, (1 - c) * same_left + c * same_right, at(p, wrap(h + 1 - 2 * c), c, y, l))
        pass_pan(part, same_left, sibling)
        pass_pan(part, same_right, sibling)

    def direct(part):
        send_inv(part, 0, up)
        send_inv(part, 1, down)
        send_pan(part)
        send_inv(part, 1, up)
        send_inv(part, 0, down)

    def split_inv(part, k):
        columns = pl.ds(pl.multiple_of(k * 512, 512), 512)
        for ri in (0, 1):
            high, low = split(inv_all[k, ri, part * TILE:(part + 1) * TILE, :])
            inv_split[0, part, ri * TILE:(ri + 1) * TILE, columns] = high
            inv_split[1, part, ri * TILE:(ri + 1) * TILE, columns] = low

    def split_pan(part, slot):
        columns = pl.ds(pl.multiple_of((slot // 2) * 512, 512), 512)
        for ri in (0, 1):
            high, low = split(pan_all[slot, ri, part * 64:(part + 1) * 64, :])
            begin = ri * TILE + (slot % 2) * 64
            pan_split[part, pl.ds(pl.multiple_of(begin, 64), 64), columns] = high
            pan_split[part, pl.ds(pl.multiple_of(begin + 256, 64), 64), columns] = low

    def split_left(part, k, source):
        rows = slice(part * 64, (part + 1) * 64)
        for ri in (0, 1):
            value = source[ri, rows, :]
            high, low = split(-value if ri else value)
            left_split[k, part * 64:(part + 1) * 64, ri * 512:(ri + 1) * 512] = high
            left_split[k, 256 + part * 64:256 + (part + 1) * 64, ri * 512:(ri + 1) * 512] = low

    other = same * (2 * h + 1 - l) + (1 - same) * 8

    def near(part):
        for ri in (0, 1):
            arrived_pan(part, own_slot, ri)
        split_pan(part, own_slot)
        for slot in (cross_left, cross_right, same_left, same_right):
            arrived_pan(part, slot, 1 - c)
            split_pan(part, slot)
        split_left(part, 1 - l, pan_all.at[other])
        arrived_inv(part, wrap(y - 1), 1)
        split_inv(part, wrap(y - 1))
        arrived_inv(part, wrap(y + 1), 0)
        split_inv(part, wrap(y + 1))

    def far(part):
        for slot in (far_left, far_right, same_far):
            arrived_pan(part, slot, c)
            pass_pan(part, slot, sibling)
        k = wrap(y + 2)
        arrived_inv(part, k, 0)
        arrived_inv(part, k, 1)
        split_inv(part, k)
        for slot in (far_left, far_right, same_far):
            arrived_pan(part, slot, 1 - c)
            split_pan(part, slot)

    real_weight = weight[0, 0]
    imag_weight = weight[0, 1]

    def sums(g, block, ks):
        from_real, from_imag = 0.0, 0.0
        for k in ks:
            columns = slice(None) if k is None else pl.ds(pl.multiple_of(k * 512, 512), 512)
            both = dot(pan_split[g, :, columns], inv_split[0, block, :, columns])
            rest = dot(pan_split[g, 0:256, columns], inv_split[1, block, :, columns])
            from_real += both[0:TILE] + both[256:384] + rest[0:TILE]
            from_imag += both[TILE:256] + both[384:512] + rest[TILE:256]
        return from_real, from_imag

    def finish(g, block, from_real, from_imag):
        real = from_real[:, 0:TILE] - from_imag[:, TILE:256]
        imag = from_imag[:, 0:TILE] + from_real[:, TILE:256]
        weighted_real = real_weight * real - imag_weight * imag
        weighted_imag = real_weight * imag + imag_weight * real
        rows = pl.ds(pl.multiple_of(g * 64, 64), 64)
        columns = pl.ds(pl.multiple_of(block * TILE, TILE), TILE)
        beside = pl.ds(pl.multiple_of(512 + block * TILE, TILE), TILE)
        for k in (0, 1):
            inner = slice(k * 64, (k + 1) * 64)
            real_part[k, rows, columns] = weighted_real[inner]
            for place, value in ((columns, weighted_real[inner]), (beside, weighted_imag[inner])):
                high, low = split(value)
                right_split[k, 0, rows, place] = high
                right_split[k, 1, rows, place] = low

    def multiply(g, block):
        finish(g, block, *sums(g, block, (None,)))

    def begin_block(place, g, block, ks):
        from_real, from_imag = sums(g, block, ks)
        begun[place, 0] = from_real
        begun[place, 1] = from_imag

    def end_block(place, g, block, ks):
        from_real, from_imag = sums(g, block, ks)
        finish(g, block, begun[place, 0] + from_real, begun[place, 1] + from_imag)

    def loop(begin, end, body):
        def step(i, _):
            body(i)
            return 0

        lax.fori_loop(begin, end, step, 0)

    def corner(part):
        loop(0, part + 1, lambda i: multiply(part, i))
        if part:
            loop(0, part, lambda i: multiply(i, part))

    raw_copy.wait()
    for g in range(PARTS):
        rows = slice(g * 64, (g + 1) * 64)
        for ri in (0, 1):
            value = raw[rows, ri, :]
            for j in range(4):
                columns = slice(j * TILE, (j + 1) * TILE)
                pan[ri, rows, columns] = value[:, columns] * mask[g // 2][j]
    pl.semaphore_wait(barrier, len(greeted))
    direct(0)
    direct(1)
    own_inv.wait()
    for part in range(PARTS):
        split_inv(part, y)
        split_left(part, l, pan)
    pass_on(0)
    direct(2)
    pass_on(1)
    pass_same(0)
    direct(3)
    pass_on(2)
    pass_same(1)
    near(0)
    far(0)
    corner(0)
    pass_on(3)
    pass_same(2)
    near(1)
    far(1)
    corner(1)
    near(2)
    far(2)
    corner(2)

    rows_first = pl.ds(pl.multiple_of(p * 48, 16), 48)
    rows_last = pl.ds(pl.multiple_of(192 + p * 16, 16), 16)

    def first_of(p_):
        return pl.ds(pl.multiple_of(p_ * 48, 16), 48)

    def last_of(p_):
        return pl.ds(pl.multiple_of(192 + p_ * 16, 16), 16)

    for p_ in poles:
        send(real_part.at[:, first_of(p_), 0:384], early.at[p], early_recv.at[p], at(p_, h, c, y, l))
    pass_same(3)
    near(3)
    there, missing = [wrap(h - 1 + l), wrap(h + l)], [wrap(h + 1 + l), wrap(h + 2 + l)]
    loop(0, 3, lambda i: begin_block(i, 3, i, there))
    loop(0, 3, lambda i: begin_block(3 + i, i, 3, [wrap(y - 1), y, wrap(y + 1)]))
    early_sum[...] = real_part[:, rows_first, 0:384]
    for p_ in poles:
        arrived(early.at[p_], early_recv.at[p_])
        early_sum[...] += early[p_]
    send(early_sum.at[1 - l], early_other, other_recv, partner)
    far(3)
    loop(0, 3, lambda i: end_block(i, 3, i, missing))
    loop(0, 3, lambda i: end_block(3 + i, i, 3, [wrap(y + 2)]))
    multiply(3, 3)

    here = ((7 - row) // 7).astype(F32)
    for o in (0, 1):
        k = l if o == 0 else 1 - l
        both = dot(left_split[k], right_split[k, 0])
        both = both[0:256] + both[256:512] + dot(left_split[k, 0:256, :], right_split[k, 1])
        for half in (0, 1):
            inner = slice(half * TILE, (half + 1) * TILE)
            tile = both[inner, inner]
            if o == 0:
                tile += here * (real_weight * diag[0, half, 0] - imag_weight * diag[0, half, 1])
            tile_part[k, half] = tile
    send(tile_part.at[:, 1 - c], tile_other, core_recv, sibling)

    me = 2 * p + l
    for p_, l_ in reducers:
        send(real_part.at[l_, last_of(p_), :], late_rows.at[me], rows_recv.at[me], at(p_, h, c, y, l_))
        send(real_part.at[l_, first_of(p_), 384:512], late_cols.at[me], cols_recv.at[me], at(p_, h, c, y, l_))

    def piece(p_):
        return pl.ds(pl.multiple_of(p_ * 32, 32), 32)

    def collect(own, buffer, recv):
        total = own
        for p_, l_ in reducers:
            k = 2 * p_ + l_
            arrived(buffer.at[k], recv.at[k])
            total += buffer[k]
        return total

    arrived(tile_other, core_recv)
    tile_sum[...] = tile_part[:, c] + tile_other[...]
    for p_, l_ in reducers:
        send(tile_sum.at[l_, piece(p_), :], tile_pieces.at[me], piece_recv.at[me], at(p_, h, c, y, l_))
    arrived(early_other, other_recv)

    def masked(total, begin, columns):
        upper = begin // TILE
        for j in columns:
            wide = slice((j - columns[0]) * TILE, (j - columns[0] + 1) * TILE)
            factor = jnp.where(upper == 0, mask[0][j], mask[1][j])
            dens[pl.ds(pl.multiple_of(begin, 16), 16), j * TILE:(j + 1) * TILE] = -factor * total[:, wide]

    for s in range(3):
        inner = slice(s * 16, (s + 1) * 16)
        masked(early_sum[l, inner, :] + early_other[inner, :], p * 48 + s * 16, (0, 1, 2))
    for p_ in poles:
        send(dens.at[rows_first, 0:384], dens.at[rows_first, 0:384], out_recv.at[p, 0], at(p_, h, c, y, l))

    tile_rows[h] = collect(tile_sum[l, piece(p), :], tile_pieces, piece_recv)
    for h_ in heights:
        send(tile_rows.at[h], tile_rows.at[h], part_recv.at[h], at(p, h_, c, y, l))
    masked(collect(real_part[l, rows_last, :], late_rows, rows_recv), 192 + p * 16, (0, 1, 2, 3))
    for p_ in poles:
        send(dens.at[rows_last, :], dens.at[rows_last, :], out_recv.at[p, 1], at(p_, h, c, y, l))
    total = collect(real_part[l, rows_first, 384:512], late_cols, cols_recv)
    for s in range(3):
        masked(total[s * 16:(s + 1) * 16], p * 48 + s * 16, (3,))
    for p_ in poles:
        send(dens.at[rows_first, 384:512], dens.at[rows_first, 384:512], out_recv.at[p, 2], at(p_, h, c, y, l))
    for h_ in heights:
        arrived(tile_rows.at[h_], part_recv.at[h_])

    def tile_of(p_, c_):
        return tiles.at[pl.ds(pl.multiple_of(c_ * TILE + p_ * 32, 32), 32), :], tile_recv.at[2 * p_ + c_]

    mine, recv = tile_of(p, c)
    mine[...] = tile_rows[0] + tile_rows[1] + tile_rows[2] + tile_rows[3]
    for p_, c_ in copies:
        send(mine, mine, recv, at(p_, h, c_, y, l))
    for p_ in poles:
        for k, target in enumerate((
            dens.at[first_of(p_), 0:384], dens.at[last_of(p_), :], dens.at[first_of(p_), 384:512],
        )):
            arrived(target, out_recv.at[p_, k])
    for p_, c_ in copies:
        arrived(*tile_of(p_, c_))
    assert slots[0] <= SENDS

    for flag, finish in waits:
        if flag is None:
            finish()
        else:
            pl.when(flag)(finish)


def shards(root_inverse, panel, diag_inverse, pole_weight, block_node, pattern):
    dma = pltpu.SemaphoreType.DMA
    vmem = pl.BlockSpec(memory_space=pltpu.VMEM)
    smem = pl.BlockSpec(memory_space=pltpu.SMEM)
    hbm = pl.BlockSpec(memory_space=pl.ANY)
    half = jnp.bfloat16
    dens, tiles = pl.pallas_call(
        kernel,
        out_shape=(jax.ShapeDtypeStruct((256, 512), F32), jax.ShapeDtypeStruct((256, TILE), F32)),
        in_specs=[hbm, hbm, vmem, smem, smem, smem],
        out_specs=(vmem, vmem),
        scratch_shapes=[
            pltpu.VMEM((256, 2, 512), F32),
            pltpu.VMEM((2, 256, 512), F32),
            pltpu.VMEM((4, 2, 512, 512), F32),
            pltpu.VMEM((9, 2, 256, 512), F32),
            pltpu.VMEM((2, 4, 256, 2048), half),
            pltpu.VMEM((4, 512, 2048), half),
            pltpu.VMEM((6, 2, TILE, 256), F32),
            pltpu.VMEM((2, 256, 512), F32),
            pltpu.VMEM((2, 512, 1024), half),
            pltpu.VMEM((2, 2, 256, 1024), half),
            pltpu.VMEM((2, 2, TILE, TILE), F32),
            pltpu.VMEM((4, 2, 48, 384), F32),
            pltpu.VMEM((2, 48, 384), F32),
            pltpu.VMEM((48, 384), F32),
            pltpu.VMEM((8, 16, 512), F32),
            pltpu.VMEM((8, 48, TILE), F32),
            pltpu.VMEM((2, TILE, TILE), F32),
            pltpu.VMEM((2, TILE, TILE), F32),
            pltpu.VMEM((8, 32, TILE), F32),
            pltpu.VMEM((4, 32, TILE), F32),
            dma((SENDS,)),
            dma((4, 2, PARTS)), dma((9, 2, PARTS)),
            dma((4,)), dma, dma((8,)), dma((8,)), dma, dma((8,)),
            dma((4,)), dma((4, 3)), dma((8,)), dma((2,)),
        ],
        compiler_params=pltpu.CompilerParams(
            collective_id=0, has_side_effects=True, vmem_limit_bytes=VMEM_LIMIT
        ),
        cost_estimate=pl.CostEstimate(flops=26_000_000_000, bytes_accessed=6_000_000, transcendentals=0),
    )(root_inverse, panel, diag_inverse, pole_weight, block_node, pattern)
    return dens, tiles.reshape(2, TILE, TILE)


def solution(mesh):
    placed = (
        P("pole", None, "row", "col"),
        P("pole", "col", None, "row"),
        P("pole", "col", None, None, None),
        P("pole", None),
        P("col"),
        P(None, "row"),
    )
    return jax.shard_map(
        shards,
        mesh=mesh,
        in_specs=placed,
        out_specs=(P("col", "row"), P("col", None, None)),
        check_vma=False,
    )
```

```python
import jax
import jax.numpy as jnp
from jax import lax
from jax.experimental import pallas as pl
from jax.experimental.pallas import tpu as pltpu
from jax.sharding import PartitionSpec as P

TILE = 128
NODES = 4
MESH = pl.DeviceIdType.MESH
HIGHEST = lax.Precision.HIGHEST
NT = (((1,), (1,)), ((), ()))
VMEM_LIMIT = 60 * 1024 * 1024
F32 = jnp.float32
PARTS = 4
SENDS = 320


def wrap(index):
    return lax.rem(index + 8, 4)


def dot(left, right, precision=None):
    return lax.dot_general(left, right, NT, precision=precision, preferred_element_type=F32)


def split(value):
    high = value.astype(jnp.bfloat16)
    return high, (value - high.astype(F32)).astype(jnp.bfloat16)


def kernel(
    inv, panel, diag, weight, node, pattern, dens, tiles,
    raw, pan, inv_all, pan_all, inv_split, pan_split, real_part, left_split, right_split, tile_part,
    early, early_sum, early_other, late_rows, tile_other, tile_sum, tile_pieces, tile_rows,
    send_sem, inv_recv, pan_recv, early_recv, other_recv, rows_recv, core_recv, piece_recv,
    part_recv, out_recv, tile_recv, own_sem,
):
    p = lax.axis_index("pole")
    row = lax.axis_index("row")
    col = lax.axis_index("col")
    h, c = row // 2, row % 2
    y, l = col // 2, col % 2
    same = 1 - (c - l) * (c - l)

    def at(p_, h_, c_, y_, l_):
        return (p_, 2 * h_ + c_, 2 * y_ + l_)

    sibling = at(p, h, 1 - c, y, l)
    partner = at(p, h, c, y, 1 - l)
    up, down = at(p, h, c, wrap(y + 1), l), at(p, h, c, wrap(y - 1), l)
    on_right, on_left = at(p, wrap(h + 1), c, y, l), at(p, wrap(h - 1), c, y, l)
    others = [(wrap(h + d), k) for d in (1, 2, 3) for k in (0, 1)] + [(h, 1 - c)]
    heights = [wrap(h + d) for d in (1, 2, 3)]
    reducers = [(wrap(p + d), (l + e) % 2) for d in range(4) for e in range(2)][1:]
    poles = [wrap(p + d) for d in (1, 2, 3)]
    copies = [(p_, c_) for p_ in poles for c_ in (c, 1 - c)] + [(p, 1 - c)]

    raw_copy = pltpu.make_async_copy(panel.at[0], raw, own_sem.at[1])
    raw_copy.start()
    own_inv = pltpu.make_async_copy(inv.at[0], inv_all.at[y], own_sem.at[0])
    own_inv.start()

    barrier = pltpu.get_barrier_semaphore()
    greeted = [up, down] + [at(p, h_, c_, y, l) for h_, c_ in others]
    greeted += [at(p, wrap(h + l), k, y, 1 - l) for k in (0, 1)]
    greeted += [at(p, wrap(h - 1 + l), k, y, 1 - l) for k in (0, 1)]
    greeted += [at(p_, h, c, y, k) for p_ in poles for k in (0, 1)]
    greeted += [at(p_, h, 1 - c, y, l) for p_ in poles]
    for device in greeted:
        pl.semaphore_signal(barrier, inc=1, device_id=device, device_id_type=MESH)

    slots = [0]
    waits = []

    def remote(source, target, recv, device, slot):
        return pltpu.make_async_remote_copy(
            src_ref=source, dst_ref=target, send_sem=send_sem.at[slot], recv_sem=recv,
            device_id=device, device_id_type=MESH,
        )

    def fresh():
        slots[0] += 1
        return slots[0] - 1

    def send(source, target, recv, device):
        copy = remote(source, target, recv, device, fresh())
        copy.start()
        waits.append((None, copy.wait_send))

    def send_if(flag, jobs):
        kept = [(job, fresh()) for job in jobs]

        @pl.when(flag)
        def _():
            for job, slot in kept:
                remote(*job, slot).start()

        def finish():
            for job, slot in kept:
                remote(*job, slot).wait_send()

        waits.append((flag, finish))

    def flush(count):
        for flag, finish in waits[:count]:
            if flag is None:
                finish()
            else:
                pl.when(flag)(finish)
        del waits[:count]

    def arrived(target, recv):
        remote(target, target, recv, sibling, 0).wait_recv()

    def entry(block, j):
        value = jnp.int32(0)
        for n in range(NODES):
            value += jnp.where(node[block] == n, pattern[n, j], 0)
        return value.astype(F32)

    mask = [[entry(block, j) for j in range(4)] for block in range(2)]

    def inv_at(k, ri, part):
        return inv_all.at[k, ri, pl.ds(part * TILE, TILE), :], inv_recv.at[k, ri, part]

    def send_inv(part, ri, device):
        send(inv.at[0, ri, pl.ds(part * TILE, TILE), :], *inv_at(y, ri, part), device)

    def pass_inv(part, k, ri, device):
        target, recv = inv_at(k, ri, part)
        send(target, target, recv, device)

    def arrived_inv(part, k, ri):
        arrived(*inv_at(k, ri, part))

    def pan_at(slot, ri, part):
        return pan_all.at[slot, ri, pl.ds(part * 64, 64), :], pan_recv.at[slot, ri, part]

    own_slot = 2 * h + l
    cross_left = 2 * wrap(h - 1 + l) + 1 - l
    cross_right = 2 * wrap(h + l) + 1 - l
    same_left = 2 * wrap(h - 1) + l
    same_right = 2 * wrap(h + 1) + l
    far_left = 2 * wrap(h - 2 + l) + 1 - l
    far_right = 2 * wrap(h + 1 + l) + 1 - l
    same_far = 2 * wrap(h + 2) + l
    behind = 2 * l - 1

    def send_pan(part):
        def job(ri, device):
            return (pan.at[ri, pl.ds(part * 64, 64), :], *pan_at(own_slot, ri, part), device)

        send_if(same == 0, [
            job(ri, at(p, wrap(h + way + l), ri, y, 1 - l)) for ri in (0, 1) for way in (0, -1)
        ])
        crossed = [
            (pan.at[ri, pl.ds(part * 64, 64), :], *pan_at(8, ri, part), partner) for ri in (0, 1)
        ]
        away = [job(ri, at(p, wrap(h + behind), ri, y, l)) for ri in (0, 1)]
        shared = [job(ri, sibling) for ri in (0, 1)]
        send_if(same == 1, crossed + away + shared)

        @pl.when(same == 1)
        def _():
            for ri in (0, 1):
                target, recv = pan_at(own_slot, ri, part)
                pltpu.make_async_copy(pan.at[ri, pl.ds(part * 64, 64), :], target, recv).start()

    def pass_pan(part, slot, device):
        target, recv = pan_at(slot, c, part)
        send(target, target, recv, device)

    def arrived_pan(part, slot, ri):
        arrived(*pan_at(slot, ri, part))

    def pass_on(part):
        @pl.when(same == 0)
        def _():
            for ri in (0, 1):
                arrived_pan(part, 8, ri)

        send_if(same == 0, [
            (pan_at(8, ri, part)[0], *pan_at(2 * h + 1 - l, ri, part), at(p, wrap(h + behind), ri, y, 1 - l))
            for ri in (0, 1)
        ])
        arrived_pan(part, cross_left, c)
        pass_pan(part, cross_left, on_right)
        pass_pan(part, cross_left, sibling)
        arrived_pan(part, cross_right, c)
        pass_pan(part, cross_right, on_left)
        pass_pan(part, cross_right, sibling)

    def inv_on(part):
        arrived_inv(part, wrap(y - 1), 0)
        pass_inv(part, wrap(y - 1), 0, up)
        arrived_inv(part, wrap(y + 1), 1)
        pass_inv(part, wrap(y + 1), 1, down)

    def pass_same(part):
        arrived_pan(part, same_left, c)
        arrived_pan(part, same_right, c)
        pass_pan(part, (1 - c) * same_left + c * same_right, at(p, wrap(h + 1 - 2 * c), c, y, l))
        pass_pan(part, same_left, sibling)
        pass_pan(part, same_right, sibling)

    def direct_inv(part):
        send_inv(part, 0, up)
        send_inv(part, 1, down)
        send_inv(part, 1, up)
        send_inv(part, 0, down)

    def split_inv(part, k):
        columns = pl.ds(pl.multiple_of(k * 512, 512), 512)
        for ri in (0, 1):
            high, low = split(inv_all[k, ri, part * TILE:(part + 1) * TILE, :])
            inv_split[0, part, ri * TILE:(ri + 1) * TILE, columns] = high
            inv_split[1, part, ri * TILE:(ri + 1) * TILE, columns] = low

    def split_pan(part, slot):
        columns = pl.ds(pl.multiple_of((slot // 2) * 512, 512), 512)
        for ri in (0, 1):
            high, low = split(pan_all[slot, ri, part * 64:(part + 1) * 64, :])
            begin = ri * TILE + (slot % 2) * 64
            pan_split[part, pl.ds(pl.multiple_of(begin, 64), 64), columns] = high
            pan_split[part, pl.ds(pl.multiple_of(begin + 256, 64), 64), columns] = low

    def split_left(part, k, source):
        rows = slice(part * 64, (part + 1) * 64)
        for ri in (0, 1):
            value = source[ri, rows, :]
            high, low = split(-value if ri else value)
            left_split[k, part * 64:(part + 1) * 64, ri * 512:(ri + 1) * 512] = high
            left_split[k, 256 + part * 64:256 + (part + 1) * 64, ri * 512:(ri + 1) * 512] = low

    other = same * (2 * h + 1 - l) + (1 - same) * 8

    def near(part):
        for ri in (0, 1):
            arrived_pan(part, own_slot, ri)
        split_pan(part, own_slot)
        for slot in (cross_left, cross_right, same_left, same_right):
            arrived_pan(part, slot, 1 - c)
            split_pan(part, slot)
        split_left(part, 1 - l, pan_all.at[other])

    def far(part):
        for slot in (far_left, far_right, same_far):
            arrived_pan(part, slot, c)
            pass_pan(part, slot, sibling)
        for slot in (far_left, far_right, same_far):
            arrived_pan(part, slot, 1 - c)
            split_pan(part, slot)

    def inv_done(part):
        k = wrap(y + 2)
        arrived_inv(part, wrap(y - 1), 1)
        split_inv(part, wrap(y - 1))
        arrived_inv(part, wrap(y + 1), 0)
        split_inv(part, wrap(y + 1))
        arrived_inv(part, k, 0)
        arrived_inv(part, k, 1)
        split_inv(part, k)

    real_weight = weight[0, 0]
    imag_weight = weight[0, 1]

    def join(both, rest):
        return (
            both[0:TILE] + both[256:384] + rest[0:TILE],
            both[TILE:256] + both[384:512] + rest[TILE:256],
        )

    def finish(g, block, from_real, from_imag):
        real = from_real[:, 0:TILE] - from_imag[:, TILE:256]
        imag = from_imag[:, 0:TILE] + from_real[:, TILE:256]
        weighted_real = real_weight * real - imag_weight * imag
        weighted_imag = real_weight * imag + imag_weight * real
        rows = pl.ds(pl.multiple_of(g * 64, 64), 64)
        columns = pl.ds(pl.multiple_of(block * TILE, TILE), TILE)
        beside = pl.ds(pl.multiple_of(512 + block * TILE, TILE), TILE)
        for k in (0, 1):
            inner = slice(k * 64, (k + 1) * 64)
            real_part[k, rows, columns] = weighted_real[inner]
            for place, value in ((columns, weighted_real[inner]), (beside, weighted_imag[inner])):
                high, low = split(value)
                right_split[k, 0, rows, place] = high
                right_split[k, 1, rows, place] = low

    def multiply(g, block):
        both = dot(pan_split[g], inv_split[0, block])
        rest = dot(pan_split[g, 0:256, :], inv_split[1, block])
        finish(g, block, *join(both, rest))

    def multiply_wide(pair):
        blocks = pl.ds(2 * pair, 2)
        both = dot(pan_split[3], inv_split[0, blocks].reshape(512, 2048))
        rest = dot(pan_split[3, 0:256, :], inv_split[1, blocks].reshape(512, 2048))
        for k in (0, 1):
            columns = slice(k * 256, (k + 1) * 256)
            finish(3, 2 * pair + k, *join(both[:, columns], rest[:, columns]))

    def multiply_tall():
        both = dot(pan_split[0:3].reshape(1536, 2048), inv_split[0, 3])
        rest = dot(pan_split[0:3, 0:256, :].reshape(768, 2048), inv_split[1, 3])
        for g in range(3):
            finish(g, 3, *join(both[g * 512:(g + 1) * 512], rest[g * 256:(g + 1) * 256]))

    def loop(begin, end, body):
        def step(i, _):
            body(i)
            return 0

        lax.fori_loop(begin, end, step, 0)

    def corner(part):
        loop(0, part + 1, lambda i: multiply(part, i))
        if part:
            loop(0, part, lambda i: multiply(i, part))

    raw_copy.wait()
    for g in range(PARTS):
        rows = slice(g * 64, (g + 1) * 64)
        for ri in (0, 1):
            value = raw[rows, ri, :]
            for j in range(4):
                columns = slice(j * TILE, (j + 1) * TILE)
                pan[ri, rows, columns] = value[:, columns] * mask[g // 2][j]
    pl.semaphore_wait(barrier, len(greeted))
    direct_inv(0)
    send_pan(0)
    send_pan(1)
    direct_inv(1)
    direct_inv(2)
    direct_inv(3)
    own_inv.wait()
    for part in range(PARTS):
        split_inv(part, y)
        split_left(part, l, pan)
    pass_on(0)
    inv_on(0)
    send_pan(2)
    pass_on(1)
    inv_on(1)
    pass_same(0)
    send_pan(3)
    marks = [len(waits)]
    pass_on(2)
    inv_on(2)
    pass_same(1)
    near(0)
    far(0)
    inv_on(3)
    inv_done(0)
    corner(0)
    marks.append(len(waits))
    pass_on(3)
    pass_same(2)
    near(1)
    far(1)
    inv_done(1)
    corner(1)
    flush(marks[0])
    near(2)
    far(2)
    inv_done(2)
    marks.append(len(waits) - marks[0])
    pass_same(3)
    corner(2)

    rows_first = pl.ds(pl.multiple_of(p * 48, 16), 48)
    rows_last = pl.ds(pl.multiple_of(192 + p * 16, 16), 16)

    def first_of(p_):
        return pl.ds(pl.multiple_of(p_ * 48, 16), 48)

    def last_of(p_):
        return pl.ds(pl.multiple_of(192 + p_ * 16, 16), 16)

    def send_early(k):
        columns = (slice(0, 384), slice(384, 512))[k]
        for p_ in poles:
            send(real_part.at[:, first_of(p_), columns], early.at[p, :, :, columns], early_recv.at[p, k],
                 at(p_, h, c, y, l))

    here = ((7 - row) // 7).astype(F32)

    def couple(half):
        rows = slice(half * TILE, (half + 1) * TILE)
        low_rows = slice(256 + half * TILE, 256 + (half + 1) * TILE)
        for o in (0, 1):
            k = l if o == 0 else 1 - l
            high = left_split[k, rows, :]
            tile = dot(high, right_split[k, 0, rows, :]) + dot(high, right_split[k, 1, rows, :])
            tile += dot(left_split[k, low_rows, :], right_split[k, 0, rows, :])
            if o == 0:
                tile += here * (real_weight * diag[0, half, 0] - imag_weight * diag[0, half, 1])
            tile_part[k, half] = tile

    send_early(0)
    inv_done(3)
    multiply_tall()
    send_early(1)
    couple(0)
    near(3)
    far(3)
    loop(0, 2, multiply_wide)
    couple(1)
    send(tile_part.at[:, 1 - c], tile_other, core_recv, sibling)
    early_sum[...] = real_part[:, rows_first, :]
    for p_ in poles:
        arrived(early.at[p_, :, :, 0:384], early_recv.at[p_, 0])
        arrived(early.at[p_, :, :, 384:512], early_recv.at[p_, 1])
        early_sum[...] += early[p_]
    send(early_sum.at[1 - l], early_other, other_recv, partner)

    me = 2 * p + l

    def piece(p_):
        return pl.ds(pl.multiple_of(p_ * 32, 32), 32)

    def collect(own, buffer, recv):
        total = own
        for p_, l_ in reducers:
            k = 2 * p_ + l_
            arrived(buffer.at[k], recv.at[k])
            total += buffer[k]
        return total

    arrived(tile_other, core_recv)
    tile_sum[...] = tile_part[:, c] + tile_other[...]
    for p_, l_ in reducers:
        send(tile_sum.at[l_, piece(p_), :], tile_pieces.at[me], piece_recv.at[me], at(p_, h, c, y, l_))
    for p_, l_ in reducers:
        send(real_part.at[l_, last_of(p_), :], late_rows.at[me], rows_recv.at[me], at(p_, h, c, y, l_))
    flush(marks[2])
    arrived(early_other, other_recv)

    def masked(total, begin):
        upper = begin // TILE
        for j in range(4):
            columns = slice(j * TILE, (j + 1) * TILE)
            factor = jnp.where(upper == 0, mask[0][j], mask[1][j])
            dens[pl.ds(pl.multiple_of(begin, 16), 16), columns] = -factor * total[:, columns]

    for s in range(3):
        inner = slice(s * 16, (s + 1) * 16)
        masked(early_sum[l, inner, :] + early_other[inner, :], p * 48 + s * 16)
    for p_ in poles:
        send(dens.at[rows_first, :], dens.at[rows_first, :], out_recv.at[p, 0], at(p_, h, c, y, l))

    tile_rows[h] = collect(tile_sum[l, piece(p), :], tile_pieces, piece_recv)
    for h_ in heights:
        send(tile_rows.at[h], tile_rows.at[h], part_recv.at[h], at(p, h_, c, y, l))
    masked(collect(real_part[l, rows_last, :], late_rows, rows_recv), 192 + p * 16)
    for p_ in poles:
        send(dens.at[rows_last, :], dens.at[rows_last, :], out_recv.at[p, 1], at(p_, h, c, y, l))
    flush(len(waits) - 26)
    for h_ in heights:
        arrived(tile_rows.at[h_], part_recv.at[h_])

    def tile_of(p_, c_):
        return tiles.at[pl.ds(pl.multiple_of(c_ * TILE + p_ * 32, 32), 32), :], tile_recv.at[2 * p_ + c_]

    mine, recv = tile_of(p, c)
    mine[...] = tile_rows[0] + tile_rows[1] + tile_rows[2] + tile_rows[3]
    for p_, c_ in copies:
        send(mine, mine, recv, at(p_, h, c_, y, l))
    for p_ in poles:
        arrived(dens.at[first_of(p_), :], out_recv.at[p_, 0])
        arrived(dens.at[last_of(p_), :], out_recv.at[p_, 1])
    for p_, c_ in copies:
        arrived(*tile_of(p_, c_))
    assert slots[0] <= SENDS

    flush(len(waits))


def shards(root_inverse, panel, diag_inverse, pole_weight, block_node, pattern):
    dma = pltpu.SemaphoreType.DMA
    vmem = pl.BlockSpec(memory_space=pltpu.VMEM)
    smem = pl.BlockSpec(memory_space=pltpu.SMEM)
    hbm = pl.BlockSpec(memory_space=pl.ANY)
    half = jnp.bfloat16
    dens, tiles = pl.pallas_call(
        kernel,
        out_shape=(jax.ShapeDtypeStruct((256, 512), F32), jax.ShapeDtypeStruct((256, TILE), F32)),
        in_specs=[hbm, hbm, vmem, smem, smem, smem],
        out_specs=(vmem, vmem),
        scratch_shapes=[
            pltpu.VMEM((256, 2, 512), F32),
            pltpu.VMEM((2, 256, 512), F32),
            pltpu.VMEM((4, 2, 512, 512), F32),
            pltpu.VMEM((9, 2, 256, 512), F32),
            pltpu.VMEM((2, 4, 256, 2048), half),
            pltpu.VMEM((4, 512, 2048), half),
            pltpu.VMEM((2, 256, 512), F32),
            pltpu.VMEM((2, 512, 1024), half),
            pltpu.VMEM((2, 2, 256, 1024), half),
            pltpu.VMEM((2, 2, TILE, TILE), F32),
            pltpu.VMEM((4, 2, 48, 512), F32),
            pltpu.VMEM((2, 48, 512), F32),
            pltpu.VMEM((48, 512), F32),
            pltpu.VMEM((8, 16, 512), F32),
            pltpu.VMEM((2, TILE, TILE), F32),
            pltpu.VMEM((2, TILE, TILE), F32),
            pltpu.VMEM((8, 32, TILE), F32),
            pltpu.VMEM((4, 32, TILE), F32),
            dma((SENDS,)),
            dma((4, 2, PARTS)), dma((9, 2, PARTS)),
            dma((4, 2)), dma, dma((8,)), dma, dma((8,)),
            dma((4,)), dma((4, 2)), dma((8,)), dma((2,)),
        ],
        compiler_params=pltpu.CompilerParams(
            collective_id=0, has_side_effects=True, vmem_limit_bytes=VMEM_LIMIT
        ),
        cost_estimate=pl.CostEstimate(flops=26_000_000_000, bytes_accessed=6_000_000, transcendentals=0),
    )(root_inverse, panel, diag_inverse, pole_weight, block_node, pattern)
    return dens, tiles.reshape(2, TILE, TILE)


def solution(mesh):
    placed = (
        P("pole", None, "row", "col"),
        P("pole", "col", None, "row"),
        P("pole", "col", None, None, None),
        P("pole", None),
        P("col"),
        P(None, "row"),
    )
    return jax.shard_map(
        shards,
        mesh=mesh,
        in_specs=placed,
        out_specs=(P("col", "row"), P("col", None, None)),
        check_vma=False,
    )
```

```python
import jax
import jax.numpy as jnp
from jax import lax
from jax.experimental import pallas as pl
from jax.experimental.pallas import tpu as pltpu
from jax.sharding import PartitionSpec as P

TILE = 128
NODES = 4
MESH = pl.DeviceIdType.MESH
HIGHEST = lax.Precision.HIGHEST
NT = (((1,), (1,)), ((), ()))
VMEM_LIMIT = 60 * 1024 * 1024
F32 = jnp.float32
PARTS = 4
SENDS = 320


def wrap(index):
    return lax.rem(index + 8, 4)


def dot(left, right, precision=None):
    return lax.dot_general(left, right, NT, precision=precision, preferred_element_type=F32)


def split(value):
    high = value.astype(jnp.bfloat16)
    return high, (value - high.astype(F32)).astype(jnp.bfloat16)


def kernel(
    inv, panel, diag, weight, node, pattern, dens, tiles,
    raw, pan, inv_all, pan_all, inv_split, pan_split, real_part, left_split, right_split, tile_part,
    early, early_sum, early_other, late_rows, tile_other, tile_sum, tile_pieces, tile_rows,
    send_sem, inv_recv, pan_recv, early_recv, other_recv, rows_recv, core_recv, piece_recv,
    part_recv, out_recv, tile_recv, own_sem,
):
    p = lax.axis_index("pole")
    row = lax.axis_index("row")
    col = lax.axis_index("col")
    h, c = row // 2, row % 2
    y, l = col // 2, col % 2
    same = 1 - (c - l) * (c - l)

    def at(p_, h_, c_, y_, l_):
        return (p_, 2 * h_ + c_, 2 * y_ + l_)

    sibling = at(p, h, 1 - c, y, l)
    partner = at(p, h, c, y, 1 - l)
    up, down = at(p, h, c, wrap(y + 1), l), at(p, h, c, wrap(y - 1), l)
    on_right, on_left = at(p, wrap(h + 1), c, y, l), at(p, wrap(h - 1), c, y, l)
    others = [(wrap(h + d), k) for d in (1, 2, 3) for k in (0, 1)] + [(h, 1 - c)]
    heights = [wrap(h + d) for d in (1, 2, 3)]
    reducers = [(wrap(p + d), (l + e) % 2) for d in range(4) for e in range(2)][1:]
    poles = [wrap(p + d) for d in (1, 2, 3)]
    copies = [(p_, c_) for p_ in poles for c_ in (c, 1 - c)] + [(p, 1 - c)]

    raw_copy = pltpu.make_async_copy(panel.at[0], raw, own_sem.at[1])
    raw_copy.start()
    own_inv = pltpu.make_async_copy(inv.at[0], inv_all.at[y], own_sem.at[0])
    own_inv.start()

    barrier = pltpu.get_barrier_semaphore()
    greeted = [up, down] + [at(p, h_, c_, y, l) for h_, c_ in others]
    greeted += [at(p, wrap(h + l), k, y, 1 - l) for k in (0, 1)]
    greeted += [at(p, wrap(h - 1 + l), k, y, 1 - l) for k in (0, 1)]
    greeted += [at(p_, h, c, y, k) for p_ in poles for k in (0, 1)]
    greeted += [at(p_, h, 1 - c, y, l) for p_ in poles]
    for device in greeted:
        pl.semaphore_signal(barrier, inc=1, device_id=device, device_id_type=MESH)

    slots = [0]
    waits = []

    def remote(source, target, recv, device, slot):
        return pltpu.make_async_remote_copy(
            src_ref=source, dst_ref=target, send_sem=send_sem.at[slot], recv_sem=recv,
            device_id=device, device_id_type=MESH,
        )

    def fresh():
        slots[0] += 1
        return slots[0] - 1

    def send(source, target, recv, device):
        copy = remote(source, target, recv, device, fresh())
        copy.start()
        waits.append((None, copy.wait_send))

    def send_if(flag, jobs):
        kept = [(job, fresh()) for job in jobs]

        @pl.when(flag)
        def _():
            for job, slot in kept:
                remote(*job, slot).start()

        def finish():
            for job, slot in kept:
                remote(*job, slot).wait_send()

        waits.append((flag, finish))

    def flush(count):
        for flag, finish in waits[:count]:
            if flag is None:
                finish()
            else:
                pl.when(flag)(finish)
        del waits[:count]

    def arrived(target, recv):
        remote(target, target, recv, sibling, 0).wait_recv()

    def entry(block, j):
        value = jnp.int32(0)
        for n in range(NODES):
            value += jnp.where(node[block] == n, pattern[n, j], 0)
        return value.astype(F32)

    mask = [[entry(block, j) for j in range(4)] for block in range(2)]

    def inv_at(k, ri, part):
        return inv_all.at[k, ri, pl.ds(part * TILE, TILE), :], inv_recv.at[k, ri, part]

    def send_inv(part, ri, device):
        send(inv.at[0, ri, pl.ds(part * TILE, TILE), :], *inv_at(y, ri, part), device)

    def pass_inv(part, k, ri, device):
        target, recv = inv_at(k, ri, part)
        send(target, target, recv, device)

    def arrived_inv(part, k, ri):
        arrived(*inv_at(k, ri, part))

    def pan_at(slot, ri, part):
        return pan_all.at[slot, ri, pl.ds(part * 64, 64), :], pan_recv.at[slot, ri, part]

    own_slot = 2 * h + l
    cross_left = 2 * wrap(h - 1 + l) + 1 - l
    cross_right = 2 * wrap(h + l) + 1 - l
    same_left = 2 * wrap(h - 1) + l
    same_right = 2 * wrap(h + 1) + l
    far_left = 2 * wrap(h - 2 + l) + 1 - l
    far_right = 2 * wrap(h + 1 + l) + 1 - l
    same_far = 2 * wrap(h + 2) + l
    behind = 2 * l - 1

    def send_pan(part):
        def job(ri, device):
            return (pan.at[ri, pl.ds(part * 64, 64), :], *pan_at(own_slot, ri, part), device)

        send_if(same == 0, [
            job(ri, at(p, wrap(h + way + l), ri, y, 1 - l)) for ri in (0, 1) for way in (0, -1)
        ])
        crossed = [
            (pan.at[ri, pl.ds(part * 64, 64), :], *pan_at(8, ri, part), partner) for ri in (0, 1)
        ]
        away = [job(ri, at(p, wrap(h + behind), ri, y, l)) for ri in (0, 1)]
        shared = [job(ri, sibling) for ri in (0, 1)]
        send_if(same == 1, crossed + away + shared)

        @pl.when(same == 1)
        def _():
            for ri in (0, 1):
                target, recv = pan_at(own_slot, ri, part)
                pltpu.make_async_copy(pan.at[ri, pl.ds(part * 64, 64), :], target, recv).start()

    def pass_pan(part, slot, device):
        target, recv = pan_at(slot, c, part)
        send(target, target, recv, device)

    def arrived_pan(part, slot, ri):
        arrived(*pan_at(slot, ri, part))

    def pass_on(part):
        @pl.when(same == 0)
        def _():
            for ri in (0, 1):
                arrived_pan(part, 8, ri)

        send_if(same == 0, [
            (pan_at(8, ri, part)[0], *pan_at(2 * h + 1 - l, ri, part), at(p, wrap(h + behind), ri, y, 1 - l))
            for ri in (0, 1)
        ])
        arrived_pan(part, cross_left, c)
        pass_pan(part, cross_left, on_right)
        pass_pan(part, cross_left, sibling)
        arrived_pan(part, cross_right, c)
        pass_pan(part, cross_right, on_left)
        pass_pan(part, cross_right, sibling)

    def inv_on(part):
        arrived_inv(part, wrap(y - 1), 0)
        pass_inv(part, wrap(y - 1), 0, up)
        arrived_inv(part, wrap(y + 1), 1)
        pass_inv(part, wrap(y + 1), 1, down)

    def pass_same(part):
        slot = (1 - l) * same_right + l * same_left
        arrived_pan(part, slot, c)
        pass_pan(part, slot, at(p, wrap(h + behind), c, y, l))
        pass_pan(part, slot, sibling)

    def take_same(part):
        slot = l * same_right + (1 - l) * same_left
        arrived_pan(part, slot, c)
        pass_pan(part, slot, sibling)

    def direct_inv(part):
        send_inv(part, 0, up)
        send_inv(part, 1, down)
        send_inv(part, 1, up)
        send_inv(part, 0, down)

    def split_inv(part, k):
        columns = pl.ds(pl.multiple_of(k * 512, 512), 512)
        for ri in (0, 1):
            high, low = split(inv_all[k, ri, part * TILE:(part + 1) * TILE, :])
            inv_split[0, part, ri * TILE:(ri + 1) * TILE, columns] = high
            inv_split[1, part, ri * TILE:(ri + 1) * TILE, columns] = low

    def split_pan(part, slot):
        columns = pl.ds(pl.multiple_of((slot // 2) * 512, 512), 512)
        for ri in (0, 1):
            high, low = split(pan_all[slot, ri, part * 64:(part + 1) * 64, :])
            begin = ri * TILE + (slot % 2) * 64
            pan_split[part, pl.ds(pl.multiple_of(begin, 64), 64), columns] = high
            pan_split[part, pl.ds(pl.multiple_of(begin + 256, 64), 64), columns] = low

    def split_left(part, k, source):
        rows = slice(part * 64, (part + 1) * 64)
        for ri in (0, 1):
            value = source[ri, rows, :]
            high, low = split(-value if ri else value)
            left_split[k, part * 64:(part + 1) * 64, ri * 512:(ri + 1) * 512] = high
            left_split[k, 256 + part * 64:256 + (part + 1) * 64, ri * 512:(ri + 1) * 512] = low

    other = same * (2 * h + 1 - l) + (1 - same) * 8

    def near(part):
        for ri in (0, 1):
            arrived_pan(part, own_slot, ri)
        split_pan(part, own_slot)
        for slot in (cross_left, cross_right, same_left, same_right):
            arrived_pan(part, slot, 1 - c)
            split_pan(part, slot)
        split_left(part, 1 - l, pan_all.at[other])

    def far(part):
        for slot in (far_left, far_right, same_far):
            arrived_pan(part, slot, c)
            pass_pan(part, slot, sibling)
        for slot in (far_left, far_right, same_far):
            arrived_pan(part, slot, 1 - c)
            split_pan(part, slot)

    def inv_done(part):
        k = wrap(y + 2)
        arrived_inv(part, wrap(y - 1), 1)
        split_inv(part, wrap(y - 1))
        arrived_inv(part, wrap(y + 1), 0)
        split_inv(part, wrap(y + 1))
        arrived_inv(part, k, 0)
        arrived_inv(part, k, 1)
        split_inv(part, k)

    real_weight = weight[0, 0]
    imag_weight = weight[0, 1]

    def join(both, rest):
        return (
            both[0:TILE] + both[256:384] + rest[0:TILE],
            both[TILE:256] + both[384:512] + rest[TILE:256],
        )

    def finish(g, block, from_real, from_imag):
        real = from_real[:, 0:TILE] - from_imag[:, TILE:256]
        imag = from_imag[:, 0:TILE] + from_real[:, TILE:256]
        weighted_real = real_weight * real - imag_weight * imag
        weighted_imag = real_weight * imag + imag_weight * real
        rows = pl.ds(pl.multiple_of(g * 64, 64), 64)
        columns = pl.ds(pl.multiple_of(block * TILE, TILE), TILE)
        beside = pl.ds(pl.multiple_of(512 + block * TILE, TILE), TILE)
        for k in (0, 1):
            inner = slice(k * 64, (k + 1) * 64)
            real_part[k, rows, columns] = weighted_real[inner]
            for place, value in ((columns, weighted_real[inner]), (beside, weighted_imag[inner])):
                high, low = split(value)
                right_split[k, 0, rows, place] = high
                right_split[k, 1, rows, place] = low

    def multiply(g, block):
        both = dot(pan_split[g], inv_split[0, block])
        rest = dot(pan_split[g, 0:256, :], inv_split[1, block])
        finish(g, block, *join(both, rest))

    def multiply_wide(pair):
        blocks = pl.ds(2 * pair, 2)
        both = dot(pan_split[3], inv_split[0, blocks].reshape(512, 2048))
        rest = dot(pan_split[3, 0:256, :], inv_split[1, blocks].reshape(512, 2048))
        for k in (0, 1):
            columns = slice(k * 256, (k + 1) * 256)
            finish(3, 2 * pair + k, *join(both[:, columns], rest[:, columns]))

    def multiply_tall():
        both = dot(pan_split[0:3].reshape(1536, 2048), inv_split[0, 3])
        rest = dot(pan_split[0:3, 0:256, :].reshape(768, 2048), inv_split[1, 3])
        for g in range(3):
            finish(g, 3, *join(both[g * 512:(g + 1) * 512], rest[g * 256:(g + 1) * 256]))

    def loop(begin, end, body):
        def step(i, _):
            body(i)
            return 0

        lax.fori_loop(begin, end, step, 0)

    def corner(part):
        loop(0, part + 1, lambda i: multiply(part, i))
        if part:
            loop(0, part, lambda i: multiply(i, part))

    raw_copy.wait()
    for g in range(PARTS):
        rows = slice(g * 64, (g + 1) * 64)
        for ri in (0, 1):
            value = raw[rows, ri, :]
            for j in range(4):
                columns = slice(j * TILE, (j + 1) * TILE)
                pan[ri, rows, columns] = value[:, columns] * mask[g // 2][j]
    pl.semaphore_wait(barrier, len(greeted))
    direct_inv(0)
    send_pan(0)
    send_pan(1)
    direct_inv(1)
    direct_inv(2)
    direct_inv(3)
    own_inv.wait()
    for part in range(PARTS):
        split_inv(part, y)
        split_left(part, l, pan)
    pass_on(0)
    pass_same(0)
    inv_on(0)
    send_pan(2)
    pass_on(1)
    pass_same(1)
    inv_on(1)
    take_same(0)
    send_pan(3)
    marks = [len(waits)]
    pass_on(2)
    pass_same(2)
    inv_on(2)
    take_same(1)
    near(0)
    far(0)
    inv_on(3)
    inv_done(0)
    corner(0)
    marks.append(len(waits))
    pass_on(3)
    pass_same(3)
    take_same(2)
    near(1)
    far(1)
    inv_done(1)
    corner(1)
    flush(marks[0])
    near(2)
    far(2)
    inv_done(2)
    marks.append(len(waits) - marks[0])
    corner(2)
    take_same(3)

    rows_first = pl.ds(pl.multiple_of(p * 48, 16), 48)
    rows_last = pl.ds(pl.multiple_of(192 + p * 16, 16), 16)

    def first_of(p_):
        return pl.ds(pl.multiple_of(p_ * 48, 16), 48)

    def last_of(p_):
        return pl.ds(pl.multiple_of(192 + p_ * 16, 16), 16)

    def send_early(k):
        columns = (slice(0, 384), slice(384, 512))[k]
        for p_ in poles:
            send(real_part.at[:, first_of(p_), columns], early.at[p, :, :, columns], early_recv.at[p, k],
                 at(p_, h, c, y, l))

    here = ((7 - row) // 7).astype(F32)

    def couple(half):
        rows = slice(half * TILE, (half + 1) * TILE)
        low_rows = slice(256 + half * TILE, 256 + (half + 1) * TILE)
        for o in (0, 1):
            k = l if o == 0 else 1 - l
            high = left_split[k, rows, :]
            tile = dot(high, right_split[k, 0, rows, :]) + dot(high, right_split[k, 1, rows, :])
            tile += dot(left_split[k, low_rows, :], right_split[k, 0, rows, :])
            if o == 0:
                tile += here * (real_weight * diag[0, half, 0] - imag_weight * diag[0, half, 1])
            tile_part[k, half] = tile

    send_early(0)
    inv_done(3)
    multiply_tall()
    send_early(1)
    couple(0)
    near(3)
    far(3)
    loop(0, 2, multiply_wide)
    couple(1)
    send(tile_part.at[:, 1 - c], tile_other, core_recv, sibling)
    early_sum[...] = real_part[:, rows_first, :]
    for p_ in poles:
        arrived(early.at[p_, :, :, 0:384], early_recv.at[p_, 0])
        arrived(early.at[p_, :, :, 384:512], early_recv.at[p_, 1])
        early_sum[...] += early[p_]
    send(early_sum.at[1 - l], early_other, other_recv, partner)

    me = 2 * p + l

    def piece(p_):
        return pl.ds(pl.multiple_of(p_ * 32, 32), 32)

    def collect(own, buffer, recv):
        total = own
        for p_, l_ in reducers:
            k = 2 * p_ + l_
            arrived(buffer.at[k], recv.at[k])
            total += buffer[k]
        return total

    arrived(tile_other, core_recv)
    tile_sum[...] = tile_part[:, c] + tile_other[...]
    for p_, l_ in reducers:
        send(tile_sum.at[l_, piece(p_), :], tile_pieces.at[me], piece_recv.at[me], at(p_, h, c, y, l_))
    for p_, l_ in reducers:
        send(real_part.at[l_, last_of(p_), :], late_rows.at[me], rows_recv.at[me], at(p_, h, c, y, l_))
    flush(marks[2])
    arrived(early_other, other_recv)

    def masked(total, begin):
        upper = begin // TILE
        for j in range(4):
            columns = slice(j * TILE, (j + 1) * TILE)
            factor = jnp.where(upper == 0, mask[0][j], mask[1][j])
            dens[pl.ds(pl.multiple_of(begin, 16), 16), columns] = -factor * total[:, columns]

    for s in range(3):
        inner = slice(s * 16, (s + 1) * 16)
        masked(early_sum[l, inner, :] + early_other[inner, :], p * 48 + s * 16)
    for p_ in poles:
        send(dens.at[rows_first, :], dens.at[rows_first, :], out_recv.at[p, 0], at(p_, h, c, y, l))

    tile_rows[h] = collect(tile_sum[l, piece(p), :], tile_pieces, piece_recv)
    for h_ in heights:
        send(tile_rows.at[h], tile_rows.at[h], part_recv.at[h], at(p, h_, c, y, l))
    masked(collect(real_part[l, rows_last, :], late_rows, rows_recv), 192 + p * 16)
    for p_ in poles:
        send(dens.at[rows_last, :], dens.at[rows_last, :], out_recv.at[p, 1], at(p_, h, c, y, l))
    flush(len(waits) - 26)
    for h_ in heights:
        arrived(tile_rows.at[h_], part_recv.at[h_])

    def tile_of(p_, c_):
        return tiles.at[pl.ds(pl.multiple_of(c_ * TILE + p_ * 32, 32), 32), :], tile_recv.at[2 * p_ + c_]

    mine, recv = tile_of(p, c)
    mine[...] = tile_rows[0] + tile_rows[1] + tile_rows[2] + tile_rows[3]
    for p_, c_ in copies:
        send(mine, mine, recv, at(p_, h, c_, y, l))
    for p_ in poles:
        arrived(dens.at[first_of(p_), :], out_recv.at[p_, 0])
        arrived(dens.at[last_of(p_), :], out_recv.at[p_, 1])
    for p_, c_ in copies:
        arrived(*tile_of(p_, c_))
    assert slots[0] <= SENDS

    flush(len(waits))


def shards(root_inverse, panel, diag_inverse, pole_weight, block_node, pattern):
    dma = pltpu.SemaphoreType.DMA
    vmem = pl.BlockSpec(memory_space=pltpu.VMEM)
    smem = pl.BlockSpec(memory_space=pltpu.SMEM)
    hbm = pl.BlockSpec(memory_space=pl.ANY)
    half = jnp.bfloat16
    dens, tiles = pl.pallas_call(
        kernel,
        out_shape=(jax.ShapeDtypeStruct((256, 512), F32), jax.ShapeDtypeStruct((256, TILE), F32)),
        in_specs=[hbm, hbm, vmem, smem, smem, smem],
        out_specs=(vmem, vmem),
        scratch_shapes=[
            pltpu.VMEM((256, 2, 512), F32),
            pltpu.VMEM((2, 256, 512), F32),
            pltpu.VMEM((4, 2, 512, 512), F32),
            pltpu.VMEM((9, 2, 256, 512), F32),
            pltpu.VMEM((2, 4, 256, 2048), half),
            pltpu.VMEM((4, 512, 2048), half),
            pltpu.VMEM((2, 256, 512), F32),
            pltpu.VMEM((2, 512, 1024), half),
            pltpu.VMEM((2, 2, 256, 1024), half),
            pltpu.VMEM((2, 2, TILE, TILE), F32),
            pltpu.VMEM((4, 2, 48, 512), F32),
            pltpu.VMEM((2, 48, 512), F32),
            pltpu.VMEM((48, 512), F32),
            pltpu.VMEM((8, 16, 512), F32),
            pltpu.VMEM((2, TILE, TILE), F32),
            pltpu.VMEM((2, TILE, TILE), F32),
            pltpu.VMEM((8, 32, TILE), F32),
            pltpu.VMEM((4, 32, TILE), F32),
            dma((SENDS,)),
            dma((4, 2, PARTS)), dma((9, 2, PARTS)),
            dma((4, 2)), dma, dma((8,)), dma, dma((8,)),
            dma((4,)), dma((4, 2)), dma((8,)), dma((2,)),
        ],
        compiler_params=pltpu.CompilerParams(
            collective_id=0, has_side_effects=True, vmem_limit_bytes=VMEM_LIMIT
        ),
        cost_estimate=pl.CostEstimate(flops=26_000_000_000, bytes_accessed=6_000_000, transcendentals=0),
    )(root_inverse, panel, diag_inverse, pole_weight, block_node, pattern)
    return dens, tiles.reshape(2, TILE, TILE)


def solution(mesh):
    placed = (
        P("pole", None, "row", "col"),
        P("pole", "col", None, "row"),
        P("pole", "col", None, None, None),
        P("pole", None),
        P("col"),
        P(None, "row"),
    )
    return jax.shard_map(
        shards,
        mesh=mesh,
        in_specs=placed,
        out_specs=(P("col", "row"), P("col", None, None)),
        check_vma=False,
    )
```

```python
import jax
import jax.numpy as jnp
from jax import lax
from jax.experimental import pallas as pl
from jax.experimental.pallas import tpu as pltpu
from jax.sharding import PartitionSpec as P

TILE = 128
NODES = 4
MESH = pl.DeviceIdType.MESH
HIGHEST = lax.Precision.HIGHEST
NT = (((1,), (1,)), ((), ()))
VMEM_LIMIT = 60 * 1024 * 1024
F32 = jnp.float32
PARTS = 4
SENDS = 320


def wrap(index):
    return lax.rem(index + 8, 4)


def dot(left, right, precision=None):
    return lax.dot_general(left, right, NT, precision=precision, preferred_element_type=F32)


def split(value):
    high = value.astype(jnp.bfloat16)
    return high, (value - high.astype(F32)).astype(jnp.bfloat16)


def kernel(
    inv, panel, diag, weight, node, pattern, dens, tiles,
    raw, pan, inv_all, pan_all, inv_split, pan_split, real_part, left_split, right_split, tile_part,
    early, early_sum, early_other, late_rows, tile_other, tile_sum, tile_pieces, tile_rows,
    send_sem, inv_recv, pan_recv, early_recv, other_recv, rows_recv, core_recv, piece_recv,
    part_recv, out_recv, tile_recv, own_sem,
):
    p = lax.axis_index("pole")
    row = lax.axis_index("row")
    col = lax.axis_index("col")
    h, c = row // 2, row % 2
    y, l = col // 2, col % 2
    same = 1 - (c - l) * (c - l)

    def at(p_, h_, c_, y_, l_):
        return (p_, 2 * h_ + c_, 2 * y_ + l_)

    sibling = at(p, h, 1 - c, y, l)
    partner = at(p, h, c, y, 1 - l)
    up, down = at(p, h, c, wrap(y + 1), l), at(p, h, c, wrap(y - 1), l)
    on_right, on_left = at(p, wrap(h + 1), c, y, l), at(p, wrap(h - 1), c, y, l)
    others = [(wrap(h + d), k) for d in (1, 2, 3) for k in (0, 1)] + [(h, 1 - c)]
    heights = [wrap(h + d) for d in (1, 2, 3)]
    reducers = [(wrap(p + d), (l + e) % 2) for d in range(4) for e in range(2)][1:]
    poles = [wrap(p + d) for d in (1, 2, 3)]
    copies = [(p_, c_) for p_ in poles for c_ in (c, 1 - c)] + [(p, 1 - c)]

    raw_copy = pltpu.make_async_copy(panel.at[0], raw, own_sem.at[1])
    raw_copy.start()
    own_inv = pltpu.make_async_copy(inv.at[0], inv_all.at[y], own_sem.at[0])
    own_inv.start()

    barrier = pltpu.get_barrier_semaphore()
    greeted = [up, down] + [at(p, h_, c_, y, l) for h_, c_ in others]
    greeted += [at(p, wrap(h + l), k, y, 1 - l) for k in (0, 1)]
    greeted += [at(p, wrap(h - 1 + l), k, y, 1 - l) for k in (0, 1)]
    greeted += [at(p_, h, c, y, k) for p_ in poles for k in (0, 1)]
    greeted += [at(p_, h, 1 - c, y, l) for p_ in poles]
    for device in greeted:
        pl.semaphore_signal(barrier, inc=1, device_id=device, device_id_type=MESH)

    slots = [0]
    waits = []

    def remote(source, target, recv, device, slot):
        return pltpu.make_async_remote_copy(
            src_ref=source, dst_ref=target, send_sem=send_sem.at[slot], recv_sem=recv,
            device_id=device, device_id_type=MESH,
        )

    def fresh():
        slots[0] += 1
        return slots[0] - 1

    def send(source, target, recv, device):
        copy = remote(source, target, recv, device, fresh())
        copy.start()
        waits.append((None, copy.wait_send))

    def send_if(flag, jobs):
        kept = [(job, fresh()) for job in jobs]

        @pl.when(flag)
        def _():
            for job, slot in kept:
                remote(*job, slot).start()

        def finish():
            for job, slot in kept:
                remote(*job, slot).wait_send()

        waits.append((flag, finish))

    def flush(count):
        for flag, finish in waits[:count]:
            if flag is None:
                finish()
            else:
                pl.when(flag)(finish)
        del waits[:count]

    def arrived(target, recv):
        remote(target, target, recv, sibling, 0).wait_recv()

    def entry(block, j):
        value = jnp.int32(0)
        for n in range(NODES):
            value += jnp.where(node[block] == n, pattern[n, j], 0)
        return value.astype(F32)

    mask = [[entry(block, j) for j in range(4)] for block in range(2)]

    def inv_at(k, ri, part):
        return inv_all.at[k, ri, pl.ds(part * TILE, TILE), :], inv_recv.at[k, ri, part]

    def send_inv(part, ri, device):
        send(inv.at[0, ri, pl.ds(part * TILE, TILE), :], *inv_at(y, ri, part), device)

    def pass_inv(part, k, ri, device):
        target, recv = inv_at(k, ri, part)
        send(target, target, recv, device)

    def arrived_inv(part, k, ri):
        arrived(*inv_at(k, ri, part))

    def pan_at(slot, ri, part):
        return pan_all.at[slot, ri, pl.ds(part * 64, 64), :], pan_recv.at[slot, ri, part]

    own_slot = 2 * h + l
    cross_left = 2 * wrap(h - 1 + l) + 1 - l
    cross_right = 2 * wrap(h + l) + 1 - l
    same_left = 2 * wrap(h - 1) + l
    same_right = 2 * wrap(h + 1) + l
    far_left = 2 * wrap(h - 2 + l) + 1 - l
    far_right = 2 * wrap(h + 1 + l) + 1 - l
    same_far = 2 * wrap(h + 2) + l
    behind = 2 * l - 1

    def send_pan(part):
        def job(ri, device):
            return (pan.at[ri, pl.ds(part * 64, 64), :], *pan_at(own_slot, ri, part), device)

        send_if(same == 0, [
            job(ri, at(p, wrap(h + way + l), ri, y, 1 - l)) for ri in (0, 1) for way in (0, -1)
        ])
        crossed = [
            (pan.at[ri, pl.ds(part * 64, 64), :], *pan_at(8, ri, part), partner) for ri in (0, 1)
        ]
        away = [job(ri, at(p, wrap(h + behind), ri, y, l)) for ri in (0, 1)]
        shared = [job(ri, sibling) for ri in (0, 1)]
        send_if(same == 1, crossed + away + shared)

        @pl.when(same == 1)
        def _():
            for ri in (0, 1):
                target, recv = pan_at(own_slot, ri, part)
                pltpu.make_async_copy(pan.at[ri, pl.ds(part * 64, 64), :], target, recv).start()

    def pass_pan(part, slot, device):
        target, recv = pan_at(slot, c, part)
        send(target, target, recv, device)

    def arrived_pan(part, slot, ri):
        arrived(*pan_at(slot, ri, part))

    def pass_on(part):
        @pl.when(same == 0)
        def _():
            for ri in (0, 1):
                arrived_pan(part, 8, ri)

        send_if(same == 0, [
            (pan_at(8, ri, part)[0], *pan_at(2 * h + 1 - l, ri, part), at(p, wrap(h + behind), ri, y, 1 - l))
            for ri in (0, 1)
        ])
        arrived_pan(part, cross_left, c)
        pass_pan(part, cross_left, on_right)
        pass_pan(part, cross_left, sibling)
        arrived_pan(part, cross_right, c)
        pass_pan(part, cross_right, on_left)
        pass_pan(part, cross_right, sibling)

    def inv_on(part):
        arrived_inv(part, wrap(y - 1), 0)
        pass_inv(part, wrap(y - 1), 0, up)
        arrived_inv(part, wrap(y + 1), 1)
        pass_inv(part, wrap(y + 1), 1, down)

    def pass_same(part):
        slot = (1 - l) * same_right + l * same_left
        arrived_pan(part, slot, c)
        pass_pan(part, slot, at(p, wrap(h + behind), c, y, l))
        pass_pan(part, slot, sibling)

    def take_same(part):
        slot = l * same_right + (1 - l) * same_left
        arrived_pan(part, slot, c)
        pass_pan(part, slot, sibling)

    def direct_inv(part):
        send_inv(part, 0, up)
        send_inv(part, 1, down)
        send_inv(part, 1, up)
        send_inv(part, 0, down)

    def split_inv(part, k):
        columns = pl.ds(pl.multiple_of(k * 512, 512), 512)
        for ri in (0, 1):
            high, low = split(inv_all[k, ri, part * TILE:(part + 1) * TILE, :])
            inv_split[0, part, ri * TILE:(ri + 1) * TILE, columns] = high
            inv_split[1, part, ri * TILE:(ri + 1) * TILE, columns] = low

    def split_pan(part, slot):
        columns = pl.ds(pl.multiple_of((slot // 2) * 512, 512), 512)
        for ri in (0, 1):
            high, low = split(pan_all[slot, ri, part * 64:(part + 1) * 64, :])
            begin = ri * TILE + (slot % 2) * 64
            pan_split[part, pl.ds(pl.multiple_of(begin, 64), 64), columns] = high
            pan_split[part, pl.ds(pl.multiple_of(begin + 256, 64), 64), columns] = low

    def split_left(part, k, source):
        rows = slice(part * 64, (part + 1) * 64)
        for ri in (0, 1):
            value = source[ri, rows, :]
            high, low = split(-value if ri else value)
            left_split[k, part * 64:(part + 1) * 64, ri * 512:(ri + 1) * 512] = high
            left_split[k, 256 + part * 64:256 + (part + 1) * 64, ri * 512:(ri + 1) * 512] = low

    other = same * (2 * h + 1 - l) + (1 - same) * 8

    def near(part):
        for ri in (0, 1):
            arrived_pan(part, own_slot, ri)
        split_pan(part, own_slot)
        for slot in (cross_left, cross_right, same_left, same_right):
            arrived_pan(part, slot, 1 - c)
            split_pan(part, slot)
        split_left(part, 1 - l, pan_all.at[other])

    def far(part):
        for slot in (far_left, far_right, same_far):
            arrived_pan(part, slot, c)
            pass_pan(part, slot, sibling)
        for slot in (far_left, far_right, same_far):
            arrived_pan(part, slot, 1 - c)
            split_pan(part, slot)

    def inv_done(part):
        k = wrap(y + 2)
        arrived_inv(part, wrap(y - 1), 1)
        split_inv(part, wrap(y - 1))
        arrived_inv(part, wrap(y + 1), 0)
        split_inv(part, wrap(y + 1))
        arrived_inv(part, k, 0)
        arrived_inv(part, k, 1)
        split_inv(part, k)

    real_weight = weight[0, 0]
    imag_weight = weight[0, 1]

    def join(both, rest):
        return (
            both[0:TILE] + both[256:384] + rest[0:TILE],
            both[TILE:256] + both[384:512] + rest[TILE:256],
        )

    def finish(g, block, from_real, from_imag):
        real = from_real[:, 0:TILE] - from_imag[:, TILE:256]
        imag = from_imag[:, 0:TILE] + from_real[:, TILE:256]
        weighted_real = real_weight * real - imag_weight * imag
        weighted_imag = real_weight * imag + imag_weight * real
        rows = pl.ds(pl.multiple_of(g * 64, 64), 64)
        columns = pl.ds(pl.multiple_of(block * TILE, TILE), TILE)
        beside = pl.ds(pl.multiple_of(512 + block * TILE, TILE), TILE)
        for k in (0, 1):
            inner = slice(k * 64, (k + 1) * 64)
            real_part[k, rows, columns] = weighted_real[inner]
            for place, value in ((columns, weighted_real[inner]), (beside, weighted_imag[inner])):
                high, low = split(value)
                right_split[k, 0, rows, place] = high
                right_split[k, 1, rows, place] = low

    def multiply(g, block):
        both = dot(pan_split[g], inv_split[0, block])
        rest = dot(pan_split[g, 0:256, :], inv_split[1, block])
        finish(g, block, *join(both, rest))

    def multiply_wide(pair):
        blocks = pl.ds(2 * pair, 2)
        both = dot(pan_split[3], inv_split[0, blocks].reshape(512, 2048))
        rest = dot(pan_split[3, 0:256, :], inv_split[1, blocks].reshape(512, 2048))
        for k in (0, 1):
            columns = slice(k * 256, (k + 1) * 256)
            finish(3, 2 * pair + k, *join(both[:, columns], rest[:, columns]))

    def multiply_tall():
        both = dot(pan_split[0:3].reshape(1536, 2048), inv_split[0, 3])
        rest = dot(pan_split[0:3, 0:256, :].reshape(768, 2048), inv_split[1, 3])
        for g in range(3):
            finish(g, 3, *join(both[g * 512:(g + 1) * 512], rest[g * 256:(g + 1) * 256]))

    def loop(begin, end, body):
        def step(i, _):
            body(i)
            return 0

        lax.fori_loop(begin, end, step, 0)

    def corner(part):
        loop(0, part + 1, lambda i: multiply(part, i))
        if part:
            loop(0, part, lambda i: multiply(i, part))

    def lay_out(g):
        rows = slice(g * 64, (g + 1) * 64)
        for ri in (0, 1):
            value = raw[rows, ri, :]
            for j in range(4):
                columns = slice(j * TILE, (j + 1) * TILE)
                pan[ri, rows, columns] = value[:, columns] * mask[g // 2][j]

    raw_copy.wait()
    lay_out(0)
    pl.semaphore_wait(barrier, len(greeted))
    send_pan(0)
    direct_inv(0)
    for part in range(1, PARTS):
        lay_out(part)
        if part < 3:
            send_pan(part)
    direct_inv(1)
    direct_inv(2)
    direct_inv(3)
    own_inv.wait()
    for part in range(PARTS):
        split_inv(part, y)
        split_left(part, l, pan)
    pass_on(0)
    pass_same(0)
    inv_on(0)
    send_pan(3)
    pass_on(1)
    pass_same(1)
    inv_on(1)
    take_same(0)
    marks = [len(waits)]
    pass_on(2)
    pass_same(2)
    inv_on(2)
    take_same(1)
    near(0)
    far(0)
    inv_on(3)
    inv_done(0)
    corner(0)
    marks.append(len(waits))
    pass_on(3)
    pass_same(3)
    take_same(2)
    near(1)
    far(1)
    inv_done(1)
    corner(1)
    flush(marks[0])
    near(2)
    far(2)
    inv_done(2)
    marks.append(len(waits) - marks[0])
    corner(2)
    take_same(3)

    rows_first = pl.ds(pl.multiple_of(p * 48, 16), 48)
    rows_last = pl.ds(pl.multiple_of(192 + p * 16, 16), 16)

    def first_of(p_):
        return pl.ds(pl.multiple_of(p_ * 48, 16), 48)

    def last_of(p_):
        return pl.ds(pl.multiple_of(192 + p_ * 16, 16), 16)

    def send_early(k):
        columns = (slice(0, 384), slice(384, 512))[k]
        for p_ in poles:
            send(real_part.at[:, first_of(p_), columns], early.at[p, :, :, columns], early_recv.at[p, k],
                 at(p_, h, c, y, l))

    here = ((7 - row) // 7).astype(F32)

    def couple(half):
        rows = slice(half * TILE, (half + 1) * TILE)
        low_rows = slice(256 + half * TILE, 256 + (half + 1) * TILE)
        for o in (0, 1):
            k = l if o == 0 else 1 - l
            high = left_split[k, rows, :]
            tile = dot(high, right_split[k, 0, rows, :]) + dot(high, right_split[k, 1, rows, :])
            tile += dot(left_split[k, low_rows, :], right_split[k, 0, rows, :])
            if o == 0:
                tile += here * (real_weight * diag[0, half, 0] - imag_weight * diag[0, half, 1])
            tile_part[k, half] = tile

    send_early(0)
    inv_done(3)
    multiply_tall()
    send_early(1)
    couple(0)
    near(3)
    far(3)
    loop(0, 2, multiply_wide)
    couple(1)
    send(tile_part.at[:, 1 - c], tile_other, core_recv, sibling)
    early_sum[...] = real_part[:, rows_first, :]
    for p_ in poles:
        arrived(early.at[p_, :, :, 0:384], early_recv.at[p_, 0])
        arrived(early.at[p_, :, :, 384:512], early_recv.at[p_, 1])
        early_sum[...] += early[p_]
    send(early_sum.at[1 - l], early_other, other_recv, partner)

    me = 2 * p + l

    def piece(p_):
        return pl.ds(pl.multiple_of(p_ * 32, 32), 32)

    def collect(own, buffer, recv):
        total = own
        for p_, l_ in reducers:
            k = 2 * p_ + l_
            arrived(buffer.at[k], recv.at[k])
            total += buffer[k]
        return total

    arrived(tile_other, core_recv)
    tile_sum[...] = tile_part[:, c] + tile_other[...]
    for p_, l_ in reducers:
        send(tile_sum.at[l_, piece(p_), :], tile_pieces.at[me], piece_recv.at[me], at(p_, h, c, y, l_))
    for p_, l_ in reducers:
        send(real_part.at[l_, last_of(p_), :], late_rows.at[me], rows_recv.at[me], at(p_, h, c, y, l_))
    flush(marks[2])
    arrived(early_other, other_recv)

    def masked(total, begin):
        upper = begin // TILE
        for j in range(4):
            columns = slice(j * TILE, (j + 1) * TILE)
            factor = jnp.where(upper == 0, mask[0][j], mask[1][j])
            dens[pl.ds(pl.multiple_of(begin, 16), 16), columns] = -factor * total[:, columns]

    for s in range(3):
        inner = slice(s * 16, (s + 1) * 16)
        masked(early_sum[l, inner, :] + early_other[inner, :], p * 48 + s * 16)
    for p_ in poles:
        send(dens.at[rows_first, :], dens.at[rows_first, :], out_recv.at[p, 0], at(p_, h, c, y, l))

    tile_rows[h] = collect(tile_sum[l, piece(p), :], tile_pieces, piece_recv)
    for h_ in heights:
        send(tile_rows.at[h], tile_rows.at[h], part_recv.at[h], at(p, h_, c, y, l))
    masked(collect(real_part[l, rows_last, :], late_rows, rows_recv), 192 + p * 16)
    for p_ in poles:
        send(dens.at[rows_last, :], dens.at[rows_last, :], out_recv.at[p, 1], at(p_, h, c, y, l))
    flush(len(waits) - 26)
    for h_ in heights:
        arrived(tile_rows.at[h_], part_recv.at[h_])

    def tile_of(p_, c_):
        return tiles.at[pl.ds(pl.multiple_of(c_ * TILE + p_ * 32, 32), 32), :], tile_recv.at[2 * p_ + c_]

    mine, recv = tile_of(p, c)
    mine[...] = tile_rows[0] + tile_rows[1] + tile_rows[2] + tile_rows[3]
    for p_, c_ in copies:
        send(mine, mine, recv, at(p_, h, c_, y, l))
    for p_ in poles:
        arrived(dens.at[first_of(p_), :], out_recv.at[p_, 0])
        arrived(dens.at[last_of(p_), :], out_recv.at[p_, 1])
    for p_, c_ in copies:
        arrived(*tile_of(p_, c_))
    assert slots[0] <= SENDS

    flush(len(waits))


def hand_over(dens_in, tiles_in, dens, tiles):
    dens[...] = dens_in[...]
    tiles[...] = tiles_in[...]


def shards(root_inverse, panel, diag_inverse, pole_weight, block_node, pattern):
    dma = pltpu.SemaphoreType.DMA
    vmem = pl.BlockSpec(memory_space=pltpu.VMEM)
    smem = pl.BlockSpec(memory_space=pltpu.SMEM)
    hbm = pl.BlockSpec(memory_space=pl.ANY)
    half = jnp.bfloat16
    dens, tiles = pl.pallas_call(
        kernel,
        out_shape=(jax.ShapeDtypeStruct((256, 512), F32), jax.ShapeDtypeStruct((256, TILE), F32)),
        in_specs=[hbm, hbm, vmem, smem, smem, smem],
        out_specs=(vmem, vmem),
        scratch_shapes=[
            pltpu.VMEM((256, 2, 512), F32),
            pltpu.VMEM((2, 256, 512), F32),
            pltpu.VMEM((4, 2, 512, 512), F32),
            pltpu.VMEM((9, 2, 256, 512), F32),
            pltpu.VMEM((2, 4, 256, 2048), half),
            pltpu.VMEM((4, 512, 2048), half),
            pltpu.VMEM((2, 256, 512), F32),
            pltpu.VMEM((2, 512, 1024), half),
            pltpu.VMEM((2, 2, 256, 1024), half),
            pltpu.VMEM((2, 2, TILE, TILE), F32),
            pltpu.VMEM((4, 2, 48, 512), F32),
            pltpu.VMEM((2, 48, 512), F32),
            pltpu.VMEM((48, 512), F32),
            pltpu.VMEM((8, 16, 512), F32),
            pltpu.VMEM((2, TILE, TILE), F32),
            pltpu.VMEM((2, TILE, TILE), F32),
            pltpu.VMEM((8, 32, TILE), F32),
            pltpu.VMEM((4, 32, TILE), F32),
            dma((SENDS,)),
            dma((4, 2, PARTS)), dma((9, 2, PARTS)),
            dma((4, 2)), dma, dma((8,)), dma, dma((8,)),
            dma((4,)), dma((4, 2)), dma((8,)), dma((2,)),
        ],
        compiler_params=pltpu.CompilerParams(
            collective_id=0, has_side_effects=True, vmem_limit_bytes=VMEM_LIMIT
        ),
        cost_estimate=pl.CostEstimate(flops=26_000_000_000, bytes_accessed=6_000_000, transcendentals=0),
    )(root_inverse, panel, diag_inverse, pole_weight, block_node, pattern)
    return pl.pallas_call(
        hand_over,
        out_shape=(jax.ShapeDtypeStruct((256, 512), F32), jax.ShapeDtypeStruct((2, TILE, TILE), F32)),
        in_specs=[vmem, vmem],
        out_specs=(vmem, vmem),
    )(dens, tiles.reshape(2, TILE, TILE))


def solution(mesh):
    placed = (
        P("pole", None, "row", "col"),
        P("pole", "col", None, "row"),
        P("pole", "col", None, None, None),
        P("pole", None),
        P("col"),
        P(None, "row"),
    )
    return jax.shard_map(
        shards,
        mesh=mesh,
        in_specs=placed,
        out_specs=(P("col", "row"), P("col", None, None)),
        check_vma=False,
    )
```

```python
import jax
import jax.numpy as jnp
from jax import lax
from jax.experimental import pallas as pl
from jax.experimental.pallas import tpu as pltpu
from jax.sharding import PartitionSpec as P

TILE = 128
NODES = 4
MESH = pl.DeviceIdType.MESH
HIGHEST = lax.Precision.HIGHEST
NT = (((1,), (1,)), ((), ()))
VMEM_LIMIT = 60 * 1024 * 1024
F32 = jnp.float32
PARTS = 4
SENDS = 320


def wrap(index):
    return lax.rem(index + 8, 4)


def dot(left, right, precision=None):
    return lax.dot_general(left, right, NT, precision=precision, preferred_element_type=F32)


def split(value):
    high = value.astype(jnp.bfloat16)
    return high, (value - high.astype(F32)).astype(jnp.bfloat16)


def kernel(
    inv, panel, diag, weight, node, pattern, dens, tiles,
    raw, pan, inv_all, pan_all, inv_split, pan_split, real_part, left_split, right_split, tile_part,
    early, early_sum, early_other, late_rows, tile_other, tile_sum, tile_pieces, tile_rows,
    send_sem, inv_recv, pan_recv, early_recv, other_recv, rows_recv, core_recv, piece_recv,
    part_recv, out_recv, tile_recv, own_sem,
):
    p = lax.axis_index("pole")
    row = lax.axis_index("row")
    col = lax.axis_index("col")
    h, c = row // 2, row % 2
    y, l = col // 2, col % 2
    same = 1 - (c - l) * (c - l)

    def at(p_, h_, c_, y_, l_):
        return (p_, 2 * h_ + c_, 2 * y_ + l_)

    sibling = at(p, h, 1 - c, y, l)
    partner = at(p, h, c, y, 1 - l)
    up, down = at(p, h, c, wrap(y + 1), l), at(p, h, c, wrap(y - 1), l)
    on_right, on_left = at(p, wrap(h + 1), c, y, l), at(p, wrap(h - 1), c, y, l)
    others = [(wrap(h + d), k) for d in (1, 2, 3) for k in (0, 1)] + [(h, 1 - c)]
    heights = [wrap(h + d) for d in (1, 2, 3)]
    reducers = [(wrap(p + d), (l + e) % 2) for d in range(4) for e in range(2)][1:]
    poles = [wrap(p + d) for d in (1, 2, 3)]
    copies = [(p_, c_) for p_ in poles for c_ in (c, 1 - c)] + [(p, 1 - c)]

    raw_copy = pltpu.make_async_copy(panel.at[0], raw, own_sem.at[1])
    raw_copy.start()
    own_inv = pltpu.make_async_copy(inv.at[0], inv_all.at[y], own_sem.at[0])
    own_inv.start()

    barrier = pltpu.get_barrier_semaphore()
    greeted = [up, down] + [at(p, h_, c_, y, l) for h_, c_ in others]
    greeted += [at(p, wrap(h + l), k, y, 1 - l) for k in (0, 1)]
    greeted += [at(p, wrap(h - 1 + l), k, y, 1 - l) for k in (0, 1)]
    greeted += [at(p_, h, c, y, k) for p_ in poles for k in (0, 1)]
    greeted += [at(p_, h, 1 - c, y, l) for p_ in poles]
    for device in greeted:
        pl.semaphore_signal(barrier, inc=1, device_id=device, device_id_type=MESH)

    slots = [0]
    waits = []

    def remote(source, target, recv, device, slot):
        return pltpu.make_async_remote_copy(
            src_ref=source, dst_ref=target, send_sem=send_sem.at[slot], recv_sem=recv,
            device_id=device, device_id_type=MESH,
        )

    def fresh():
        slots[0] += 1
        return slots[0] - 1

    def send(source, target, recv, device):
        copy = remote(source, target, recv, device, fresh())
        copy.start()
        waits.append((None, copy.wait_send))

    def send_if(flag, jobs):
        kept = [(job, fresh()) for job in jobs]

        @pl.when(flag)
        def _():
            for job, slot in kept:
                remote(*job, slot).start()

        def finish():
            for job, slot in kept:
                remote(*job, slot).wait_send()

        waits.append((flag, finish))

    def flush(count):
        for flag, finish in waits[:count]:
            if flag is None:
                finish()
            else:
                pl.when(flag)(finish)
        del waits[:count]

    def arrived(target, recv):
        remote(target, target, recv, sibling, 0).wait_recv()

    def entry(block, j):
        value = jnp.int32(0)
        for n in range(NODES):
            value += jnp.where(node[block] == n, pattern[n, j], 0)
        return value.astype(F32)

    mask = [[entry(block, j) for j in range(4)] for block in range(2)]

    def inv_at(k, ri, part):
        return inv_all.at[k, ri, pl.ds(part * TILE, TILE), :], inv_recv.at[k, ri, part]

    def send_inv(part, ri, device):
        send(inv.at[0, ri, pl.ds(part * TILE, TILE), :], *inv_at(y, ri, part), device)

    def pass_inv(part, k, ri, device):
        target, recv = inv_at(k, ri, part)
        send(target, target, recv, device)

    def arrived_inv(part, k, ri):
        arrived(*inv_at(k, ri, part))

    def pan_at(slot, ri, part):
        return pan_all.at[slot, ri, pl.ds(part * 64, 64), :], pan_recv.at[slot, ri, part]

    own_slot = 2 * h + l
    cross_left = 2 * wrap(h - 1 + l) + 1 - l
    cross_right = 2 * wrap(h + l) + 1 - l
    same_left = 2 * wrap(h - 1) + l
    same_right = 2 * wrap(h + 1) + l
    far_left = 2 * wrap(h - 2 + l) + 1 - l
    far_right = 2 * wrap(h + 1 + l) + 1 - l
    same_far = 2 * wrap(h + 2) + l
    behind = 2 * l - 1

    def send_pan(part):
        def job(ri, device):
            return (pan.at[ri, pl.ds(part * 64, 64), :], *pan_at(own_slot, ri, part), device)

        send_if(same == 0, [
            job(ri, at(p, wrap(h + way + l), ri, y, 1 - l)) for ri in (0, 1) for way in (0, -1)
        ])
        crossed = [
            (pan.at[ri, pl.ds(part * 64, 64), :], *pan_at(8, ri, part), partner) for ri in (0, 1)
        ]
        away = [job(ri, at(p, wrap(h + behind), ri, y, l)) for ri in (0, 1)]
        shared = [job(ri, sibling) for ri in (0, 1)]
        send_if(same == 1, crossed + away + shared)

        @pl.when(same == 1)
        def _():
            for ri in (0, 1):
                target, recv = pan_at(own_slot, ri, part)
                pltpu.make_async_copy(pan.at[ri, pl.ds(part * 64, 64), :], target, recv).start()

    def pass_pan(part, slot, device):
        target, recv = pan_at(slot, c, part)
        send(target, target, recv, device)

    def arrived_pan(part, slot, ri):
        arrived(*pan_at(slot, ri, part))

    def pass_on(part):
        @pl.when(same == 0)
        def _():
            for ri in (0, 1):
                arrived_pan(part, 8, ri)

        send_if(same == 0, [
            (pan_at(8, ri, part)[0], *pan_at(2 * h + 1 - l, ri, part), at(p, wrap(h + behind), ri, y, 1 - l))
            for ri in (0, 1)
        ])
        arrived_pan(part, cross_left, c)
        pass_pan(part, cross_left, on_right)
        pass_pan(part, cross_left, sibling)
        arrived_pan(part, cross_right, c)
        pass_pan(part, cross_right, on_left)
        pass_pan(part, cross_right, sibling)

    def inv_on(part):
        arrived_inv(part, wrap(y - 1), 0)
        pass_inv(part, wrap(y - 1), 0, up)
        arrived_inv(part, wrap(y + 1), 1)
        pass_inv(part, wrap(y + 1), 1, down)

    def pass_same(part):
        slot = (1 - l) * same_right + l * same_left
        arrived_pan(part, slot, c)
        pass_pan(part, slot, at(p, wrap(h + behind), c, y, l))
        pass_pan(part, slot, sibling)

    def take_same(part):
        slot = l * same_right + (1 - l) * same_left
        arrived_pan(part, slot, c)
        pass_pan(part, slot, sibling)

    def direct_inv(part):
        send_inv(part, 0, up)
        send_inv(part, 1, down)
        send_inv(part, 1, up)
        send_inv(part, 0, down)

    def split_inv(part, k):
        columns = pl.ds(pl.multiple_of(k * 512, 512), 512)
        for ri in (0, 1):
            high, low = split(inv_all[k, ri, part * TILE:(part + 1) * TILE, :])
            inv_split[0, part, ri * TILE:(ri + 1) * TILE, columns] = high
            inv_split[1, part, ri * TILE:(ri + 1) * TILE, columns] = low

    def split_pan(part, slot):
        columns = pl.ds(pl.multiple_of((slot // 2) * 512, 512), 512)
        for ri in (0, 1):
            high, low = split(pan_all[slot, ri, part * 64:(part + 1) * 64, :])
            begin = ri * TILE + (slot % 2) * 64
            pan_split[part, pl.ds(pl.multiple_of(begin, 64), 64), columns] = high
            pan_split[part, pl.ds(pl.multiple_of(begin + 256, 64), 64), columns] = low

    def split_left(part, k, source):
        rows = slice(part * 64, (part + 1) * 64)
        for ri in (0, 1):
            value = source[ri, rows, :]
            high, low = split(-value if ri else value)
            left_split[k, part * 64:(part + 1) * 64, ri * 512:(ri + 1) * 512] = high
            left_split[k, 256 + part * 64:256 + (part + 1) * 64, ri * 512:(ri + 1) * 512] = low

    other = same * (2 * h + 1 - l) + (1 - same) * 8

    def near(part):
        for ri in (0, 1):
            arrived_pan(part, own_slot, ri)
        split_pan(part, own_slot)
        for slot in (cross_left, cross_right, same_left, same_right):
            arrived_pan(part, slot, 1 - c)
            split_pan(part, slot)
        split_left(part, 1 - l, pan_all.at[other])

    def far(part):
        for slot in (far_left, far_right, same_far):
            arrived_pan(part, slot, c)
            pass_pan(part, slot, sibling)
        for slot in (far_left, far_right, same_far):
            arrived_pan(part, slot, 1 - c)
            split_pan(part, slot)

    def inv_done(part):
        k = wrap(y + 2)
        arrived_inv(part, wrap(y - 1), 1)
        split_inv(part, wrap(y - 1))
        arrived_inv(part, wrap(y + 1), 0)
        split_inv(part, wrap(y + 1))
        arrived_inv(part, k, 0)
        arrived_inv(part, k, 1)
        split_inv(part, k)

    real_weight = weight[0, 0]
    imag_weight = weight[0, 1]

    def join(both, rest):
        return (
            both[0:TILE] + both[256:384] + rest[0:TILE],
            both[TILE:256] + both[384:512] + rest[TILE:256],
        )

    def finish(g, block, from_real, from_imag):
        real = from_real[:, 0:TILE] - from_imag[:, TILE:256]
        imag = from_imag[:, 0:TILE] + from_real[:, TILE:256]
        weighted_real = real_weight * real - imag_weight * imag
        weighted_imag = real_weight * imag + imag_weight * real
        rows = pl.ds(pl.multiple_of(g * 64, 64), 64)
        columns = pl.ds(pl.multiple_of(block * TILE, TILE), TILE)
        beside = pl.ds(pl.multiple_of(512 + block * TILE, TILE), TILE)
        for k in (0, 1):
            inner = slice(k * 64, (k + 1) * 64)
            real_part[k, rows, columns] = weighted_real[inner]
            for place, value in ((columns, weighted_real[inner]), (beside, weighted_imag[inner])):
                high, low = split(value)
                right_split[k, 0, rows, place] = high
                right_split[k, 1, rows, place] = low

    def multiply(g, block):
        both = dot(pan_split[g], inv_split[0, block])
        rest = dot(pan_split[g, 0:256, :], inv_split[1, block])
        finish(g, block, *join(both, rest))

    def multiply_wide(pair):
        blocks = pl.ds(2 * pair, 2)
        both = dot(pan_split[3], inv_split[0, blocks].reshape(512, 2048))
        rest = dot(pan_split[3, 0:256, :], inv_split[1, blocks].reshape(512, 2048))
        for k in (0, 1):
            columns = slice(k * 256, (k + 1) * 256)
            finish(3, 2 * pair + k, *join(both[:, columns], rest[:, columns]))

    def multiply_tall():
        both = dot(pan_split[0:3].reshape(1536, 2048), inv_split[0, 3])
        rest = dot(pan_split[0:3, 0:256, :].reshape(768, 2048), inv_split[1, 3])
        for g in range(3):
            finish(g, 3, *join(both[g * 512:(g + 1) * 512], rest[g * 256:(g + 1) * 256]))

    def loop(begin, end, body):
        def step(i, _):
            body(i)
            return 0

        lax.fori_loop(begin, end, step, 0)

    def corner(part):
        loop(0, part + 1, lambda i: multiply(part, i))
        if part:
            loop(0, part, lambda i: multiply(i, part))

    def lay_out(g):
        rows = slice(g * 64, (g + 1) * 64)
        for ri in (0, 1):
            value = raw[rows, ri, :]
            for j in range(4):
                columns = slice(j * TILE, (j + 1) * TILE)
                pan[ri, rows, columns] = value[:, columns] * mask[g // 2][j]

    raw_copy.wait()
    lay_out(0)
    pl.semaphore_wait(barrier, len(greeted))
    send_pan(0)
    direct_inv(0)
    for part in range(1, PARTS):
        lay_out(part)
        if part < 3:
            send_pan(part)
    direct_inv(1)
    direct_inv(2)
    direct_inv(3)
    own_inv.wait()
    for part in range(PARTS):
        split_inv(part, y)
        split_left(part, l, pan)
    pass_on(0)
    pass_same(0)
    inv_on(0)
    send_pan(3)
    pass_on(1)
    pass_same(1)
    inv_on(1)
    take_same(0)
    marks = [len(waits)]
    pass_on(2)
    pass_same(2)
    inv_on(2)
    take_same(1)
    near(0)
    far(0)
    inv_on(3)
    inv_done(0)
    corner(0)
    marks.append(len(waits))
    pass_on(3)
    pass_same(3)
    take_same(2)
    near(1)
    far(1)
    inv_done(1)
    corner(1)
    flush(marks[0])
    near(2)
    far(2)
    inv_done(2)
    marks.append(len(waits) - marks[0])
    corner(2)
    take_same(3)

    rows_first = pl.ds(pl.multiple_of(p * 48, 16), 48)
    rows_last = pl.ds(pl.multiple_of(192 + p * 16, 16), 16)

    def first_of(p_):
        return pl.ds(pl.multiple_of(p_ * 48, 16), 48)

    def last_of(p_):
        return pl.ds(pl.multiple_of(192 + p_ * 16, 16), 16)

    def send_early(k):
        columns = (slice(0, 384), slice(384, 512))[k]
        for p_ in poles:
            send(real_part.at[:, first_of(p_), columns], early.at[p, :, :, columns], early_recv.at[p, k],
                 at(p_, h, c, y, l))

    here = ((7 - row) // 7).astype(F32)

    def couple(half):
        rows = slice(half * TILE, (half + 1) * TILE)
        low_rows = slice(256 + half * TILE, 256 + (half + 1) * TILE)
        for o in (0, 1):
            k = l if o == 0 else 1 - l
            high = left_split[k, rows, :]
            tile = dot(high, right_split[k, 0, rows, :]) + dot(high, right_split[k, 1, rows, :])
            tile += dot(left_split[k, low_rows, :], right_split[k, 0, rows, :])
            if o == 0:
                tile += here * (real_weight * diag[0, half, 0] - imag_weight * diag[0, half, 1])
            tile_part[k, half] = tile

    send_early(0)
    inv_done(3)
    multiply_tall()
    send_early(1)
    couple(0)
    near(3)
    far(3)
    loop(0, 2, multiply_wide)
    couple(1)
    send(tile_part.at[:, 1 - c], tile_other, core_recv, sibling)
    early_sum[...] = real_part[:, rows_first, :]
    for p_ in poles:
        arrived(early.at[p_, :, :, 0:384], early_recv.at[p_, 0])
        arrived(early.at[p_, :, :, 384:512], early_recv.at[p_, 1])
        early_sum[...] += early[p_]
    send(early_sum.at[1 - l], early_other, other_recv, partner)

    me = 2 * p + l

    def piece(p_):
        return pl.ds(pl.multiple_of(p_ * 32, 32), 32)

    def collect(own, buffer, recv):
        total = own
        for p_, l_ in reducers:
            k = 2 * p_ + l_
            arrived(buffer.at[k], recv.at[k])
            total += buffer[k]
        return total

    arrived(tile_other, core_recv)
    tile_sum[...] = tile_part[:, c] + tile_other[...]
    for p_, l_ in reducers:
        send(tile_sum.at[l_, piece(p_), :], tile_pieces.at[me], piece_recv.at[me], at(p_, h, c, y, l_))
    for p_, l_ in reducers:
        send(real_part.at[l_, last_of(p_), :], late_rows.at[me], rows_recv.at[me], at(p_, h, c, y, l_))
    arrived(early_other, other_recv)

    def masked(total, begin):
        upper = begin // TILE
        for j in range(4):
            columns = slice(j * TILE, (j + 1) * TILE)
            factor = jnp.where(upper == 0, mask[0][j], mask[1][j])
            dens[pl.ds(pl.multiple_of(begin, 16), 16), columns] = -factor * total[:, columns]

    for s in range(3):
        inner = slice(s * 16, (s + 1) * 16)
        masked(early_sum[l, inner, :] + early_other[inner, :], p * 48 + s * 16)
    for p_ in poles:
        send(dens.at[rows_first, :], dens.at[rows_first, :], out_recv.at[p, 0], at(p_, h, c, y, l))

    tile_rows[h] = collect(tile_sum[l, piece(p), :], tile_pieces, piece_recv)
    for h_ in heights:
        send(tile_rows.at[h], tile_rows.at[h], part_recv.at[h], at(p, h_, c, y, l))
    flush(marks[2])
    masked(collect(real_part[l, rows_last, :], late_rows, rows_recv), 192 + p * 16)
    for p_ in poles:
        send(dens.at[rows_last, :], dens.at[rows_last, :], out_recv.at[p, 1], at(p_, h, c, y, l))
    flush(len(waits) - 26)
    for h_ in heights:
        arrived(tile_rows.at[h_], part_recv.at[h_])

    def tile_of(p_, c_):
        return tiles.at[pl.ds(pl.multiple_of(c_ * TILE + p_ * 32, 32), 32), :], tile_recv.at[2 * p_ + c_]

    mine, recv = tile_of(p, c)
    mine[...] = tile_rows[0] + tile_rows[1] + tile_rows[2] + tile_rows[3]
    for p_, c_ in copies:
        send(mine, mine, recv, at(p_, h, c_, y, l))
    for p_ in poles:
        arrived(dens.at[first_of(p_), :], out_recv.at[p_, 0])
        arrived(dens.at[last_of(p_), :], out_recv.at[p_, 1])
    for p_, c_ in copies:
        arrived(*tile_of(p_, c_))
    assert slots[0] <= SENDS

    flush(len(waits))


def hand_over(dens_in, tiles_in, dens, tiles, sems):
    copies = [
        pltpu.make_async_copy(dens_in, dens, sems.at[0]),
        pltpu.make_async_copy(tiles_in, tiles, sems.at[1]),
    ]
    for copy in copies:
        copy.start()
    for copy in copies:
        copy.wait()


def shards(root_inverse, panel, diag_inverse, pole_weight, block_node, pattern):
    dma = pltpu.SemaphoreType.DMA
    vmem = pl.BlockSpec(memory_space=pltpu.VMEM)
    smem = pl.BlockSpec(memory_space=pltpu.SMEM)
    hbm = pl.BlockSpec(memory_space=pl.ANY)
    half = jnp.bfloat16
    dens, tiles = pl.pallas_call(
        kernel,
        out_shape=(jax.ShapeDtypeStruct((256, 512), F32), jax.ShapeDtypeStruct((256, TILE), F32)),
        in_specs=[hbm, hbm, vmem, smem, smem, smem],
        out_specs=(vmem, vmem),
        scratch_shapes=[
            pltpu.VMEM((256, 2, 512), F32),
            pltpu.VMEM((2, 256, 512), F32),
            pltpu.VMEM((4, 2, 512, 512), F32),
            pltpu.VMEM((9, 2, 256, 512), F32),
            pltpu.VMEM((2, 4, 256, 2048), half),
            pltpu.VMEM((4, 512, 2048), half),
            pltpu.VMEM((2, 256, 512), F32),
            pltpu.VMEM((2, 512, 1024), half),
            pltpu.VMEM((2, 2, 256, 1024), half),
            pltpu.VMEM((2, 2, TILE, TILE), F32),
            pltpu.VMEM((4, 2, 48, 512), F32),
            pltpu.VMEM((2, 48, 512), F32),
            pltpu.VMEM((48, 512), F32),
            pltpu.VMEM((8, 16, 512), F32),
            pltpu.VMEM((2, TILE, TILE), F32),
            pltpu.VMEM((2, TILE, TILE), F32),
            pltpu.VMEM((8, 32, TILE), F32),
            pltpu.VMEM((4, 32, TILE), F32),
            dma((SENDS,)),
            dma((4, 2, PARTS)), dma((9, 2, PARTS)),
            dma((4, 2)), dma, dma((8,)), dma, dma((8,)),
            dma((4,)), dma((4, 2)), dma((8,)), dma((2,)),
        ],
        compiler_params=pltpu.CompilerParams(
            collective_id=0, has_side_effects=True, vmem_limit_bytes=VMEM_LIMIT
        ),
        cost_estimate=pl.CostEstimate(flops=26_000_000_000, bytes_accessed=6_000_000, transcendentals=0),
    )(root_inverse, panel, diag_inverse, pole_weight, block_node, pattern)
    return pl.pallas_call(
        hand_over,
        out_shape=(jax.ShapeDtypeStruct((256, 512), F32), jax.ShapeDtypeStruct((2, TILE, TILE), F32)),
        in_specs=[vmem, vmem],
        out_specs=(hbm, hbm),
        scratch_shapes=[dma((2,))],
    )(dens, tiles.reshape(2, TILE, TILE))


def solution(mesh):
    placed = (
        P("pole", None, "row", "col"),
        P("pole", "col", None, "row"),
        P("pole", "col", None, None, None),
        P("pole", None),
        P("col"),
        P(None, "row"),
    )
    return jax.shard_map(
        shards,
        mesh=mesh,
        in_specs=placed,
        out_specs=(P("col", "row"), P("col", None, None)),
        check_vma=False,
    )
```
